32 devices in a mesh: win: 2 (over y), tmpl: 4 (over z), sta: 4 (over x, core).
Axes of the slice: x: 2, y: 2, z: 4, core: 2. Of those that a mesh axis runs over, the one named last changes fastest.
Arguments:
- records: bfloat16 [384, 3, 3584], P(('win', 'sta')), parts along dimension 0
- templates: bfloat16 [16, 192, 3, 100], P(('win', 'tmpl'), 'sta'), parts along dimension 0
- channel_valid: int32 [16, 192, 3], P(('win', 'tmpl'), 'sta'), parts along dimension 0, may hold values from 0 to 1, as said below
- shifts: int32 [16, 192], P(('win', 'tmpl'), 'sta'), parts along dimension 0, may hold values from 0 to 412, as said below
- hypo_id: int32 [16], P(('win', 'tmpl')), parts along dimension 0, may hold values from 0 to 255
- hypo_xyz: float32 [3, 256], replicated, may hold values from -1 to 1
Outputs:
- peak_score: float32 [6144], P(('win', 'sta')), parts along dimension 0
- evidence: float32 [6144], P(('win', 'sta')), parts along dimension 0
- location: float32 [3, 6144], P(None, ('win', 'sta')), parts along dimension 1
The draws below stay inside these ranges and needn't reach their ends.
There are 2 independent parts, one for each index of `win`. The reference program is written for one: setup_inputs(seed, part) draws one part's arguments, and reference() takes and returns one part's arrays. A program takes and returns all parts, laid end to end along the dimension named above; an argument that names none is the same for every part. Nothing has to cross between parts.
Inputs may be any that keep to these rules, and one draw needn't show every extreme that they name: `channel_valid`: every template has all three channels of at least one station valid. `shifts`: for every template some station has moveout 0.
All inputs are finite; a program needn't handle non-finite values.
Results may differ from the reference program's by a relative error of at most 0.0044.
Values sent between devices are 32-bit elements; how exact they have to be, the bound alone decides.
A program may use at most 64 MiB of HBM per device.

```python
import math
import jax
import jax.numpy as jnp
from jax import lax

STATIONS = 192
TAPS = 100
PAD = 512
HYPOS = 256
TMPL_DEV = 2
SAMPLES = 3072
TEMPLATES = 8
RECORD = 3584


def draw_shifts(key, part):
    base = jax.random.randint(jax.random.fold_in(key, 11), (TEMPLATES, STATIONS), 0, PAD - TAPS + 1)
    row_index = jnp.arange(TEMPLATES)[:, None]
    col_index = jnp.arange(STATIONS)[None, :]
    farthest = col_index == row_index * 7 % STATIONS
    nearest = col_index == (row_index * 7 + 1) % STATIONS
    return jnp.where(farthest, PAD - TAPS, jnp.where(nearest, 0, base)).astype(jnp.int32)


def template_shapes(key):
    wave_key = jax.random.fold_in(key, 21)
    amp_key = jax.random.fold_in(key, 22)
    wave = jax.random.normal(wave_key, (TEMPLATES, STATIONS, 3, TAPS), jnp.float32)
    amplitude = jnp.exp(jax.random.uniform(amp_key, (TEMPLATES, STATIONS, 3, 1), jnp.float32, 0.0, 2.3026))
    return wave * amplitude


def draw_templates(key, part):
    return template_shapes(key).astype(jnp.bfloat16)


def draw_channel_valid(key, part):
    tickets = jax.random.randint(jax.random.fold_in(key, 31), (TEMPLATES, STATIONS, 3), 0, 1000)
    limits = 150 + 800 * jnp.arange(STATIONS) // STATIONS
    homes = jax.random.randint(jax.random.fold_in(key, 32), (TEMPLATES, 1), 0, STATIONS)
    at_home = (jnp.arange(STATIONS)[None, :] == homes)[:, :, None]
    chosen = (tickets < limits[None, :, None]) | at_home
    return chosen.astype(jnp.int32)


def draw_records(key, part):
    noise = jax.random.truncated_normal(jax.random.fold_in(key, 51), -4.0, 4.0, (STATIONS, 3, RECORD), jnp.float32)
    gains = jnp.exp(jax.random.uniform(jax.random.fold_in(key, 52), (STATIONS, 3, 1), jnp.float32, 0.0, 2.3026))
    envelope_blocks = jnp.exp(jax.random.uniform(jax.random.fold_in(key, 53), (STATIONS, 1, RECORD // 64 + 1), jnp.float32, 0.0, 1.3863))
    envelope = envelope_blocks[:, :, jnp.arange(RECORD) // 64]
    traces = noise * gains * envelope
    return traces.astype(jnp.bfloat16)


def plant(array, key, smallest, high):
    longest = array.shape.index(max(array.shape))
    spots = []
    for shift in (0, 1):
        where = [jax.random.randint(jax.random.fold_in(key, axis), (), 0, length) for axis, length in enumerate(array.shape)]
        where[longest] = (where[longest] + shift) % array.shape[longest]
        spots.append(tuple(where))
    return array.at[spots[0]].set(smallest).at[spots[1]].set(high)


def setup_inputs(seed: int = 0, part: int = 0) -> dict:
    key_list = jax.random.split(jax.random.key(seed), 7)
    own_keys = jax.random.split(jax.random.fold_in(key_list[6], part), 7)
    records = draw_records(jax.random.fold_in(jax.random.fold_in(key_list[6], part), 71), part)
    templates = draw_templates(jax.random.fold_in(jax.random.fold_in(key_list[6], part), 71), part)
    channel_valid = draw_channel_valid(jax.random.fold_in(jax.random.fold_in(key_list[6], part), 71), part)
    shifts = draw_shifts(jax.random.fold_in(jax.random.fold_in(key_list[6], part), 71), part)
    hypo_id = plant(jax.random.randint(own_keys[4], (TEMPLATES,), 0, HYPOS), jax.random.fold_in(own_keys[4], 1), 0, HYPOS - 1).astype(jnp.int32)
    hypo_xyz = jnp.clip(jax.random.uniform(key_list[5], (3, HYPOS), jnp.float32, -1.0, 1.0), -1.0, 1.0)
    return dict(records=records, templates=templates, channel_valid=channel_valid, shifts=shifts, hypo_id=hypo_id, hypo_xyz=hypo_xyz)


sharpness = 400.0
epsilon = 1e-06

def normed_templates(templates):
    wide = templates.astype(jnp.float32)
    power = lax.optimization_barrier(jnp.mean(wide * wide, axis=-1, keepdims=True))
    return (wide / (wide.shape[-1] * jnp.sqrt(power + epsilon))).astype(jnp.bfloat16)

def window_norm(channels, taps_len):
    squares = channels.astype(jnp.float32) * channels.astype(jnp.float32)
    ones_kernel = jnp.ones((squares.shape[0], 1, taps_len), jnp.float32)
    energy = lax.conv_general_dilated(squares[None], ones_kernel, (1,), 'VALID', dimension_numbers=('NCH', 'OIH', 'NCH'), feature_group_count=squares.shape[0], precision=lax.Precision.HIGHEST)[0]
    return jnp.sqrt(energy / taps_len + epsilon)

def block_trace(records_blk, normed_blk, valid_blk, shift_blk, out_length):
    sta_count, comp_count, in_length = records_blk.shape
    tpl_count, taps_len = (normed_blk.shape[0], normed_blk.shape[-1])
    chan_count = sta_count * comp_count
    channels = records_blk.reshape(chan_count, in_length)
    kernel = jnp.transpose(normed_blk, (1, 2, 0, 3)).reshape(chan_count * tpl_count, 1, taps_len)
    raw_corr = lax.conv_general_dilated(channels[None], kernel, (1,), 'VALID', dimension_numbers=('NCH', 'OIH', 'NCH'), feature_group_count=chan_count, preferred_element_type=jnp.float32)[0]
    norms = window_norm(channels, taps_len)
    weights = jnp.transpose(valid_blk, (1, 2, 0)).reshape(chan_count, tpl_count).astype(jnp.float32)
    scaled = raw_corr.reshape(chan_count, tpl_count, -1) / norms[:, None, :] * weights[:, :, None]
    station_sum = lax.optimization_barrier(jnp.sum(scaled.reshape(sta_count, comp_count, tpl_count, -1), axis=1))

    def align(row, offset):
        return lax.dynamic_slice_in_dim(row, offset.astype(jnp.int32), out_length)
    aligned = jax.vmap(jax.vmap(align))(station_sum, shift_blk.T)
    return lax.optimization_barrier(jnp.sum(aligned, axis=0))

def correlate(records, normed, channel_valid, shifts, out_length):
    sta_total = records.shape[0]
    block_size = math.gcd(sta_total, 8)

    def accumulate(totals, block_index):
        first_row = (block_index * block_size).astype(jnp.int32)
        part_records = lax.dynamic_slice_in_dim(records, first_row, block_size, 0)
        part_normed = lax.dynamic_slice_in_dim(normed, first_row, block_size, 1)
        part_valid = lax.dynamic_slice_in_dim(channel_valid, first_row, block_size, 1)
        part_shift = lax.dynamic_slice_in_dim(shifts, first_row, block_size, 1)
        return (totals + block_trace(part_records, part_normed, part_valid, part_shift, out_length), None)
    start_value = jnp.zeros((normed.shape[0], out_length), jnp.float32)
    totals, unused = lax.scan(accumulate, start_value, jnp.arange(sta_total // block_size, dtype=jnp.int32))
    return totals

def reference(records, templates, channel_valid, shifts, hypo_id, hypo_xyz):
    normed = normed_templates(templates)

    def per_block(block_index):
        first_tpl = (block_index * TMPL_DEV).astype(jnp.int32)
        block_normed = lax.dynamic_slice_in_dim(normed, first_tpl, TMPL_DEV, 0)
        block_valid = lax.dynamic_slice_in_dim(channel_valid, first_tpl, TMPL_DEV, 0)
        block_shift = lax.dynamic_slice_in_dim(shifts, first_tpl, TMPL_DEV, 0)
        return correlate(records, block_normed, block_valid, block_shift, SAMPLES)
    traces = lax.map(per_block, jnp.arange(TEMPLATES // TMPL_DEV, dtype=jnp.int32)).reshape(TEMPLATES, SAMPLES)
    counts = lax.optimization_barrier(jnp.sum(channel_valid, axis=(1, 2))).astype(jnp.float32)
    scores = sharpness * (traces / counts[:, None])
    peak_score = lax.optimization_barrier(jnp.max(scores, axis=0))
    weights = jnp.exp(scores - peak_score[None, :])
    totals = lax.optimization_barrier(jnp.sum(weights, axis=0))
    evidence = peak_score + jnp.log(totals)
    positions = hypo_xyz[:, hypo_id]
    located = jnp.dot(positions, weights, precision=lax.Precision.HIGHEST)
    location = located / totals[None, :]
    return (peak_score, evidence, location)
```

```python
import functools
import math

import jax
import jax.numpy as jnp
from jax import lax
from jax.experimental import pallas as pl
from jax.experimental.pallas import tpu as pltpu
from jax.sharding import PartitionSpec as P

SAMPLES = 3072

sharpness = 400.0
epsilon = 1e-06
LANES = 128


def first_rows(templates, channel_valid):
    wide = templates.astype(jnp.float32)
    taps = wide.shape[-1]
    power = jnp.mean(wide * wide, axis=-1, keepdims=True)
    normed = (wide / (taps * jnp.sqrt(power + epsilon))).astype(jnp.bfloat16).astype(jnp.float32)
    normed = normed * channel_valid.astype(jnp.float32)[..., None]
    row = jnp.concatenate(
        [
            normed[..., :1],
            jnp.zeros(normed.shape[:-1] + (LANES - taps,), jnp.float32),
            jnp.flip(normed[..., 1:], -1),
        ],
        axis=-1,
    )
    return jnp.transpose(row, (1, 2, 0, 3)).reshape(-1, LANES)


def trace_kernel(
    taps, group, unroll, shift_ref, x_ref, w_ref, out_ref, xs, xw, rn, scr
):
    stations, comps, samples = x_ref.shape
    temps = out_ref.shape[0]
    out_rows = out_ref.shape[1]
    rows = samples // LANES
    prows = -(-(rows + 1) // 8) * 8
    srows = comps * prows
    j_id = lax.broadcasted_iota(jnp.int32, (LANES, LANES), 0)
    i_id = lax.broadcasted_iota(jnp.int32, (LANES, LANES), 1)
    upper = j_id >= i_id
    gap = j_id - i_id
    band = jnp.concatenate(
        [
            jnp.where((gap >= 0) & (gap < taps), 1.0, 0.0),
            jnp.where(gap + LANES < taps, 1.0, 0.0),
        ],
        axis=0,
    ).astype(jnp.bfloat16)

    def prepare(g, _):
        base = pl.multiple_of(g * (group * srows), 8)
        for k in range(group):
            wave = x_ref[g * group + k].astype(jnp.float32)
            for c in range(comps):
                xs[pl.ds(base + k * srows + c * prows + prows - 8, 8), :] = jnp.zeros(
                    (8, LANES), jnp.float32
                )
            for r in range(rows):
                xs[pl.ds(base + k * srows + r, comps, stride=prows), :] = wave[
                    :, r * LANES : (r + 1) * LANES
                ]
        count = group * srows
        here = xs[pl.ds(base, count), :]
        after = xs[pl.ds(base + 1, count), :]
        window = jnp.concatenate([here, after], axis=1)
        xw[pl.ds(base, count), :] = window.astype(jnp.bfloat16)
        square = window * window
        high = square.astype(jnp.bfloat16)
        low = (square - high.astype(jnp.float32)).astype(jnp.bfloat16)
        energy = jnp.dot(high, band, preferred_element_type=jnp.float32) + jnp.dot(
            low, band, preferred_element_type=jnp.float32
        )
        rn[pl.ds(base, count), :] = lax.rsqrt(energy * (1.0 / taps) + epsilon)
        return 0

    xs[pl.ds(stations * srows, 8), :] = jnp.zeros((8, LANES), jnp.float32)
    lax.fori_loop(0, stations // group, prepare, 0)

    lane = lax.broadcasted_iota(jnp.int32, (out_rows, LANES), 1)

    def one_station(s, slot):
        sums = [None] * temps
        for c in range(comps):
            base = pl.multiple_of((s * comps + c) * prows, 16)
            data = xw[pl.ds(base, prows), :]
            inverse = rn[pl.ds(base, prows), :]
            tiles = []
            for t in range(temps):
                row = w_ref[pl.ds((s * comps + c) * temps + t, 1), :]
                ring = pltpu.roll(
                    jnp.broadcast_to(row, (LANES, LANES)), 0, 1, stride=1, stride_axis=0
                )
                tiles.append(
                    jnp.concatenate(
                        [jnp.where(upper, ring, 0.0), jnp.where(upper, 0.0, ring)], axis=0
                    ).astype(jnp.bfloat16)
                )
            raw = jnp.dot(
                data, jnp.concatenate(tiles, axis=1), preferred_element_type=jnp.float32
            )
            for t in range(temps):
                term = raw[:, t * LANES : (t + 1) * LANES] * inverse
                sums[t] = term if sums[t] is None else sums[t] + term
        for t in range(temps):
            shift = shift_ref[t, s]
            whole = lax.shift_right_logical(shift, 7)
            part = lax.bitwise_and(shift, LANES - 1)
            scr[slot, t] = pltpu.roll(
                sums[t], lax.bitwise_and(LANES - part, LANES - 1), 1
            )
            near = scr[slot, t, pl.ds(whole, out_rows), :]
            far = scr[slot, t, pl.ds(whole + 1, out_rows), :]
            out_ref[t] += jnp.where(lane < LANES - part, near, far)

    out_ref[...] = jnp.zeros_like(out_ref)

    def some_stations(g, _):
        for k in range(unroll):
            one_station(g * unroll + k, k)
        return 0

    lax.fori_loop(0, stations // unroll, some_stations, 0)


def partial_traces(records, templates, channel_valid, shifts):
    stations, comps, samples = records.shape
    temps, taps = templates.shape[0], templates.shape[-1]
    rows = samples // LANES
    prows = -(-(rows + 1) // 8) * 8
    total = stations * comps * prows
    group = math.gcd(stations, 4)
    unroll = math.gcd(stations, 2)
    return pl.pallas_call(
        functools.partial(trace_kernel, taps, group, unroll),
        out_shape=jax.ShapeDtypeStruct((temps, SAMPLES // LANES, LANES), jnp.float32),
        in_specs=[
            pl.BlockSpec(memory_space=pltpu.SMEM),
            pl.BlockSpec(memory_space=pltpu.VMEM),
            pl.BlockSpec(memory_space=pltpu.VMEM),
        ],
        out_specs=pl.BlockSpec(memory_space=pltpu.VMEM),
        scratch_shapes=[
            pltpu.VMEM((total + 8, LANES), jnp.float32),
            pltpu.VMEM((total, 2 * LANES), jnp.bfloat16),
            pltpu.VMEM((total, LANES), jnp.float32),
            pltpu.VMEM((unroll, temps, prows, LANES), jnp.float32),
        ],
        compiler_params=pltpu.CompilerParams(vmem_limit_bytes=40 * 2**20),
        name="traces",
    )(shifts, records, first_rows(templates, channel_valid))


def on_device(records, templates, channel_valid, shifts, hypo_id, hypo_xyz):
    partial_value = partial_traces(records, templates, channel_valid, shifts)
    temps = partial_value.shape[0]
    own_count = jnp.sum(channel_valid, axis=(1, 2)).astype(jnp.float32)
    traces = lax.psum_scatter(
        partial_value.reshape(temps, SAMPLES), "sta", scatter_dimension=1, tiled=True
    )
    counts = lax.psum(own_count, "sta")
    places = hypo_xyz[:, hypo_id]
    scores = lax.all_gather(sharpness * (traces / counts[:, None]), "tmpl", axis=0, tiled=True)
    places = lax.all_gather(places, "tmpl", axis=1, tiled=True)
    best = jnp.max(scores, axis=0)
    weights = jnp.exp(scores - best[None, :])
    totals = jnp.sum(weights, axis=0)
    located = jnp.sum(places[:, :, None] * weights[None], axis=1)
    return (best, best + jnp.log(totals), located / totals[None, :])


def solution(mesh):
    return jax.shard_map(
        on_device,
        mesh=mesh,
        in_specs=(
            P(("win", "sta"), None, None),
            P(("win", "tmpl"), "sta", None, None),
            P(("win", "tmpl"), "sta", None),
            P(("win", "tmpl"), "sta"),
            P(("win", "tmpl")),
            P(),
        ),
        out_specs=(P(("win", "sta")), P(("win", "sta")), P(None, ("win", "sta"))),
        check_vma=False,
    )
```

```python
import functools
import math

import jax
import jax.numpy as jnp
from jax import lax
from jax.experimental import pallas as pl
from jax.experimental.pallas import tpu as pltpu
from jax.sharding import PartitionSpec as P

SAMPLES = 3072

sharpness = 400.0
epsilon = 1e-06
LANES = 128


def trace_kernel(
    taps, group, unroll, shift_ref, valid_ref, hypo_ref, place_ref, x_ref, w_ref,
    out_ref, xs, xw, rn, ws, acc, scr
):
    comps, stations, samples = x_ref.shape
    chunks, temps, chunk_rows = out_ref.shape[:3]
    out_rows = acc.shape[1]
    rows = samples // LANES
    prows = -(-(rows + 1) // 8) * 8
    srows = comps * prows
    j_id = lax.broadcasted_iota(jnp.int32, (LANES, LANES), 0)
    i_id = lax.broadcasted_iota(jnp.int32, (LANES, LANES), 1)
    upper = j_id >= i_id
    gap = j_id - i_id
    band = jnp.concatenate(
        [
            jnp.where((gap >= 0) & (gap < taps), 1.0, 0.0),
            jnp.where(gap + LANES < taps, 1.0, 0.0),
        ],
        axis=0,
    ).astype(jnp.bfloat16)

    k_id = lax.broadcasted_iota(jnp.int32, (taps, LANES), 0)
    l_id = lax.broadcasted_iota(jnp.int32, (taps, LANES), 1)
    turn = jnp.where(lax.bitwise_and(k_id + l_id, LANES - 1) == 0, 1.0, 0.0).astype(jnp.bfloat16)
    for c in range(comps):
        for t in range(temps):
            wide = w_ref[t, c].astype(jnp.float32)
            power = jnp.sum(wide * wide, axis=-1, keepdims=True) / taps
            normed = (wide / (taps * jnp.sqrt(power + epsilon))).astype(jnp.bfloat16)
            ws[pl.ds((c * temps + t) * stations, stations), :] = jnp.dot(
                normed, turn, preferred_element_type=jnp.float32
            )

    xs[pl.ds(stations * srows, 8), :] = jnp.zeros((8, LANES), jnp.float32)

    def prepare(g, _):
        base = pl.multiple_of(g * (group * srows), 8)
        first = pl.multiple_of(g * group, group)
        for k in range(group * comps):
            xs[pl.ds(base + k * prows + prows - 8, 8), :] = jnp.zeros((8, LANES), jnp.float32)
        for c in range(comps):
            wave = x_ref[c, pl.ds(first, group), :].astype(jnp.float32)
            for r in range(rows):
                xs[pl.ds(base + c * prows + r, group, stride=srows), :] = wave[
                    :, r * LANES : (r + 1) * LANES
                ]
        count = group * srows
        here = xs[pl.ds(base, count), :]
        after = xs[pl.ds(base + 1, count), :]
        window = jnp.concatenate([here, after], axis=1)
        xw[pl.ds(base, count), :] = window.astype(jnp.bfloat16)
        square = window * window
        high = square.astype(jnp.bfloat16)
        low = (square - high.astype(jnp.float32)).astype(jnp.bfloat16)
        energy = jnp.dot(high, band, preferred_element_type=jnp.float32) + jnp.dot(
            low, band, preferred_element_type=jnp.float32
        )
        rn[pl.ds(base, count), :] = lax.rsqrt(energy * (1.0 / taps) + epsilon)
        return 0

    lax.fori_loop(0, stations // group, prepare, 0)

    lane = lax.broadcasted_iota(jnp.int32, (out_rows, LANES), 1)

    def one_station(s, slot, counts):
        sums = [None] * temps
        counts = list(counts)
        for c in range(comps):
            base = pl.multiple_of((s * comps + c) * prows, 16)
            data = xw[pl.ds(base, prows), :]
            inverse = rn[pl.ds(base, prows), :]
            tiles = []
            for t in range(temps):
                valid = valid_ref[c, t, s]
                counts[t] = counts[t] + valid
                row = ws[pl.ds((c * temps + t) * stations + s, 1), :] * valid.astype(jnp.float32)
                ring = pltpu.roll(
                    jnp.broadcast_to(row, (LANES, LANES)), 0, 1, stride=1, stride_axis=0
                )
                tiles.append(
                    jnp.concatenate(
                        [jnp.where(upper, ring, 0.0), jnp.where(upper, 0.0, ring)], axis=0
                    ).astype(jnp.bfloat16)
                )
            raw = jnp.dot(
                data, jnp.concatenate(tiles, axis=1), preferred_element_type=jnp.float32
            )
            for t in range(temps):
                term = raw[:, t * LANES : (t + 1) * LANES] * inverse
                sums[t] = term if sums[t] is None else sums[t] + term
        for t in range(temps):
            shift = shift_ref[t, s]
            whole = lax.shift_right_logical(shift, 7)
            part = lax.bitwise_and(shift, LANES - 1)
            scr[slot, t] = pltpu.roll(
                sums[t], lax.bitwise_and(LANES - part, LANES - 1), 1
            )
            near = scr[slot, t, pl.ds(whole, out_rows), :]
            far = scr[slot, t, pl.ds(whole + 1, out_rows), :]
            acc[t] += jnp.where(lane < LANES - part, near, far)
        return tuple(counts)

    acc[...] = jnp.zeros_like(acc)

    def some_stations(g, counts):
        for k in range(unroll):
            counts = one_station(g * unroll + k, k, counts)
        return counts

    counts = lax.fori_loop(
        0, stations // unroll, some_stations, tuple(jnp.int32(0) for _ in range(temps))
    )

    share = out_rows // chunks
    axes, hypos = place_ref.shape
    h_id = lax.broadcasted_iota(jnp.int32, (axes, hypos), 1)
    row_id = lax.broadcasted_iota(jnp.int32, (axes, LANES), 0)
    col_id = lax.broadcasted_iota(jnp.int32, (axes, LANES), 1)
    for t in range(temps):
        place = jnp.sum(
            jnp.where(h_id == hypo_ref[t], place_ref[...], 0.0), axis=1, keepdims=True
        )
        place_row = jnp.sum(jnp.where(row_id == col_id, place, 0.0), axis=0, keepdims=True)
        count_row = jnp.full((1, LANES), counts[t].astype(jnp.float32))
        for b in range(chunks):
            out_ref[b, t, pl.ds(0, share), :] = acc[t, pl.ds(b * share, share), :]
            out_ref[b, t, pl.ds(share, 1), :] = count_row
            out_ref[b, t, pl.ds(share + 1, 1), :] = place_row
            if chunk_rows > share + 2:
                out_ref[b, t, pl.ds(share + 2, chunk_rows - share - 2), :] = jnp.zeros(
                    (chunk_rows - share - 2, LANES), jnp.float32
                )


def partial_traces(records, templates, channel_valid, shifts, hypo_id, hypo_xyz):
    stations, comps, samples = records.shape
    temps, taps = templates.shape[0], templates.shape[-1]
    rows = samples // LANES
    prows = -(-(rows + 1) // 8) * 8
    total = stations * comps * prows
    group = math.gcd(stations, 16)
    unroll = math.gcd(stations, 2)
    chunks = lax.axis_size("sta")
    out_rows = SAMPLES // LANES
    chunk_rows = -(-(out_rows // chunks + 2) // 8) * 8
    smem = pl.BlockSpec(memory_space=pltpu.SMEM)
    vmem = pl.BlockSpec(memory_space=pltpu.VMEM)
    return pl.pallas_call(
        functools.partial(trace_kernel, taps, group, unroll),
        out_shape=jax.ShapeDtypeStruct((chunks, temps, chunk_rows, LANES), jnp.float32),
        in_specs=[smem, smem, smem, vmem, vmem, vmem],
        out_specs=vmem,
        scratch_shapes=[
            pltpu.VMEM((total + 8, LANES), jnp.float32),
            pltpu.VMEM((total, 2 * LANES), jnp.bfloat16),
            pltpu.VMEM((total, LANES), jnp.float32),
            pltpu.VMEM((comps * temps * stations, LANES), jnp.float32),
            pltpu.VMEM((temps, out_rows, LANES), jnp.float32),
            pltpu.VMEM((unroll, temps, prows, LANES), jnp.float32),
        ],
        compiler_params=pltpu.CompilerParams(vmem_limit_bytes=40 * 2**20),
        name="traces",
    )(
        shifts,
        jnp.transpose(channel_valid, (2, 0, 1)),
        hypo_id,
        hypo_xyz,
        jnp.transpose(records, (1, 0, 2)),
        jnp.transpose(templates, (0, 2, 1, 3)),
    )


def combine_kernel(
    share, axes, n_sta, n_tmpl, part_ref, best_ref, evidence_ref, place_ref,
    summed, held, score_held, send_a, recv_a, send_b, recv_b
):
    temps = part_ref.shape[1]
    sta, tmpl = lax.axis_index("sta"), lax.axis_index("tmpl")
    barrier = pltpu.get_barrier_semaphore()
    for k in range(1, n_sta):
        pl.semaphore_signal(
            barrier, inc=1, device_id={"sta": lax.rem(sta + k, n_sta)},
            device_id_type=pl.DeviceIdType.MESH,
        )
    for k in range(1, n_tmpl):
        pl.semaphore_signal(
            barrier, inc=1, device_id={"tmpl": lax.rem(tmpl + k, n_tmpl)},
            device_id_type=pl.DeviceIdType.MESH,
        )
    pl.semaphore_wait(barrier, n_sta + n_tmpl - 2)

    copies = []
    for k in range(1, n_sta):
        peer = lax.rem(sta + k, n_sta)
        copies.append(
            pltpu.make_async_remote_copy(
                src_ref=part_ref.at[peer],
                dst_ref=held.at[k - 1],
                send_sem=send_a.at[k - 1],
                recv_sem=recv_a.at[k - 1],
                device_id={"sta": peer},
                device_id_type=pl.DeviceIdType.MESH,
            )
        )
        copies[-1].start()
    whole = part_ref[sta]
    for k, copy in enumerate(copies):
        copy.wait_recv()
        whole = whole + held[k]
    row_id = lax.broadcasted_iota(jnp.int32, whole.shape, 1)
    counts = whole[:, share : share + 1, :]
    summed[...] = jnp.where(
        row_id < share, sharpness * (whole / counts), part_ref[sta]
    )
    later = []
    for k in range(1, n_tmpl):
        peer = lax.rem(tmpl + k, n_tmpl)
        later.append(
            pltpu.make_async_remote_copy(
                src_ref=summed,
                dst_ref=score_held.at[k - 1],
                send_sem=send_b.at[k - 1],
                recv_sem=recv_b.at[k - 1],
                device_id={"tmpl": peer},
                device_id_type=pl.DeviceIdType.MESH,
            )
        )
        later[-1].start()
    for copy in copies:
        copy.wait_send()
    blocks = [summed[...]]
    for k, copy in enumerate(later):
        copy.wait_recv()
        blocks.append(score_held[k])
    pieces = [block[t] for block in blocks for t in range(temps)]
    best = pieces[0]
    for piece in pieces[1:]:
        best = jnp.maximum(best, piece)
    total = jnp.zeros_like(best)
    sums = [jnp.zeros_like(best) for _ in range(axes)]
    for piece in pieces:
        weight = jnp.exp(piece - best)
        total = total + weight
        for j in range(axes):
            sums[j] = sums[j] + weight * piece[share + 1 : share + 2, j : j + 1]
    best_ref[...] = best[:share]
    evidence_ref[...] = (best + jnp.log(total))[:share]
    for j in range(axes):
        located = sums[j] / total
        for r in range(share):
            place_ref[pl.ds(j, 1), pl.ds(r * LANES, LANES)] = located[r : r + 1]
    for copy in later:
        copy.wait_send()


def on_device(records, templates, channel_valid, shifts, hypo_id, hypo_xyz):
    part = partial_traces(records, templates, channel_valid, shifts, hypo_id, hypo_xyz)
    n_sta, n_tmpl = lax.axis_size("sta"), lax.axis_size("tmpl")
    axes = hypo_xyz.shape[0]
    block = part.shape[1:]
    share = SAMPLES // LANES // n_sta
    vmem = pl.BlockSpec(memory_space=pltpu.VMEM)
    best, evidence, location = pl.pallas_call(
        functools.partial(combine_kernel, share, axes, n_sta, n_tmpl),
        out_shape=(
            jax.ShapeDtypeStruct((share, LANES), jnp.float32),
            jax.ShapeDtypeStruct((share, LANES), jnp.float32),
            jax.ShapeDtypeStruct((axes, share * LANES), jnp.float32),
        ),
        in_specs=[vmem],
        out_specs=(vmem, vmem, vmem),
        scratch_shapes=[
            pltpu.VMEM(block, jnp.float32),
            pltpu.VMEM((n_sta - 1,) + block, jnp.float32),
            pltpu.VMEM((n_tmpl - 1,) + block, jnp.float32),
            pltpu.SemaphoreType.DMA((n_sta - 1,)),
            pltpu.SemaphoreType.DMA((n_sta - 1,)),
            pltpu.SemaphoreType.DMA((n_tmpl - 1,)),
            pltpu.SemaphoreType.DMA((n_tmpl - 1,)),
        ],
        compiler_params=pltpu.CompilerParams(collective_id=0, has_side_effects=True),
        name="combine",
    )(part)
    return (best.reshape(-1), evidence.reshape(-1), location)


def solution(mesh):
    return jax.shard_map(
        on_device,
        mesh=mesh,
        in_specs=(
            P(("win", "sta"), None, None),
            P(("win", "tmpl"), "sta", None, None),
            P(("win", "tmpl"), "sta", None),
            P(("win", "tmpl"), "sta"),
            P(("win", "tmpl")),
            P(),
        ),
        out_specs=(P(("win", "sta")), P(("win", "sta")), P(None, ("win", "sta"))),
        check_vma=False,
    )
```

```python
import functools
import math

import jax
import jax.numpy as jnp
from jax import lax
from jax.experimental import pallas as pl
from jax.experimental.pallas import tpu as pltpu
from jax.sharding import PartitionSpec as P

SAMPLES = 3072

sharpness = 400.0
epsilon = 1e-06
LANES = 128


def trace_kernel(
    taps, group, unroll, n_sta, n_tmpl,
    shift_hbm, valid_hbm, hypo_hbm, place_hbm, x_hbm, w_hbm, out_ref,
    shift_ref, valid_ref, hypo_ref, place_ref, x_ref, w_ref,
    xs, xw, rn, ws, acc, scr, part_ref, held,
    sem_in, sem_x, send_a, recv_a, send_b, recv_b
):
    comps, stations, samples = x_ref.shape
    chunks, temps, chunk_rows = part_ref.shape[:3]
    sta, tmpl = lax.axis_index("sta"), lax.axis_index("tmpl")
    barrier = pltpu.get_barrier_semaphore()
    for axis, me, size in (("sta", sta, n_sta), ("tmpl", tmpl, n_tmpl)):
        for k in range(1, size):
            pl.semaphore_signal(
                barrier, inc=1, device_id={axis: lax.rem(me + k, size)},
                device_id_type=pl.DeviceIdType.MESH,
            )
    w_copy = pltpu.make_async_copy(w_hbm, w_ref, sem_in.at[0])
    w_copy.start()
    x_copies = []
    for g in range(stations // group):
        span = pl.ds(g * group, group)
        x_copies.append(
            pltpu.make_async_copy(x_hbm.at[:, span, :], x_ref.at[:, span, :], sem_x.at[g])
        )
        x_copies[-1].start()
    small = []
    for n, (src, dst) in enumerate(
        (
            (shift_hbm, shift_ref), (valid_hbm, valid_ref),
            (hypo_hbm, hypo_ref), (place_hbm, place_ref),
        )
    ):
        small.append(pltpu.make_async_copy(src, dst, sem_in.at[n + 1]))
        small[-1].start()
    out_rows = acc.shape[1]
    rows = samples // LANES
    prows = -(-(rows + 1) // 8) * 8
    srows = comps * prows
    j_id = lax.broadcasted_iota(jnp.int32, (LANES, LANES), 0)
    i_id = lax.broadcasted_iota(jnp.int32, (LANES, LANES), 1)
    upper = j_id >= i_id
    gap = j_id - i_id
    band = jnp.concatenate(
        [
            jnp.where((gap >= 0) & (gap < taps), 1.0, 0.0),
            jnp.where(gap + LANES < taps, 1.0, 0.0),
        ],
        axis=0,
    ).astype(jnp.bfloat16)

    k_id = lax.broadcasted_iota(jnp.int32, (taps, LANES), 0)
    l_id = lax.broadcasted_iota(jnp.int32, (taps, LANES), 1)
    turn = jnp.where(lax.bitwise_and(k_id + l_id, LANES - 1) == 0, 1.0, 0.0).astype(jnp.bfloat16)
    w_copy.wait()
    for c in range(comps):
        for t in range(temps):
            wide = w_ref[t, c].astype(jnp.float32)
            power = jnp.sum(wide * wide, axis=-1, keepdims=True) / taps
            normed = (wide / (taps * jnp.sqrt(power + epsilon))).astype(jnp.bfloat16)
            ws[pl.ds((c * temps + t) * stations, stations), :] = jnp.dot(
                normed, turn, preferred_element_type=jnp.float32
            )

    xs[pl.ds(stations * srows, 8), :] = jnp.zeros((8, LANES), jnp.float32)

    def prepare(g, _):
        base = g * (group * srows)
        first = g * group
        for k in range(group * comps):
            xs[pl.ds(base + k * prows + prows - 8, 8), :] = jnp.zeros((8, LANES), jnp.float32)
        for c in range(comps):
            wave = x_ref[c, pl.ds(first, group), :].astype(jnp.float32)
            for r in range(rows):
                xs[pl.ds(base + c * prows + r, group, stride=srows), :] = wave[
                    :, r * LANES : (r + 1) * LANES
                ]
        count = group * srows
        here = xs[pl.ds(base, count), :]
        after = xs[pl.ds(base + 1, count), :]
        window = jnp.concatenate([here, after], axis=1)
        xw[pl.ds(base, count), :] = window.astype(jnp.bfloat16)
        square = window * window
        high = square.astype(jnp.bfloat16)
        low = (square - high.astype(jnp.float32)).astype(jnp.bfloat16)
        energy = jnp.dot(high, band, preferred_element_type=jnp.float32) + jnp.dot(
            low, band, preferred_element_type=jnp.float32
        )
        rn[pl.ds(base, count), :] = lax.rsqrt(energy * (1.0 / taps) + epsilon)
        return 0

    for g, copy in enumerate(x_copies):
        copy.wait()
        prepare(g, 0)
    for copy in small:
        copy.wait()

    lane = lax.broadcasted_iota(jnp.int32, (out_rows, LANES), 1)

    def one_station(s, slot, counts):
        sums = [None] * temps
        counts = list(counts)
        for c in range(comps):
            base = pl.multiple_of((s * comps + c) * prows, 16)
            data = xw[pl.ds(base, prows), :]
            inverse = rn[pl.ds(base, prows), :]
            tiles = []
            for t in range(temps):
                valid = valid_ref[c, t, s]
                counts[t] = counts[t] + valid
                row = ws[pl.ds((c * temps + t) * stations + s, 1), :] * valid.astype(jnp.float32)
                ring = pltpu.roll(
                    jnp.broadcast_to(row, (LANES, LANES)), 0, 1, stride=1, stride_axis=0
                )
                tiles.append(
                    jnp.concatenate(
                        [jnp.where(upper, ring, 0.0), jnp.where(upper, 0.0, ring)], axis=0
                    ).astype(jnp.bfloat16)
                )
            raw = jnp.dot(
                data, jnp.concatenate(tiles, axis=1), preferred_element_type=jnp.float32
            )
            for t in range(temps):
                term = raw[:, t * LANES : (t + 1) * LANES] * inverse
                sums[t] = term if sums[t] is None else sums[t] + term
        for t in range(temps):
            shift = shift_ref[t, s]
            whole = lax.shift_right_logical(shift, 7)
            part = lax.bitwise_and(shift, LANES - 1)
            scr[slot, t] = pltpu.roll(
                sums[t], lax.bitwise_and(LANES - part, LANES - 1), 1
            )
            near = scr[slot, t, pl.ds(whole, out_rows), :]
            far = scr[slot, t, pl.ds(whole + 1, out_rows), :]
            acc[t] += jnp.where(lane < LANES - part, near, far)
        return tuple(counts)

    acc[...] = jnp.zeros_like(acc)

    def some_stations(g, counts):
        for k in range(unroll):
            counts = one_station(g * unroll + k, k, counts)
        return counts

    counts = lax.fori_loop(
        0, stations // unroll, some_stations, tuple(jnp.int32(0) for _ in range(temps))
    )

    share = out_rows // chunks
    axes, hypos = place_ref.shape
    h_id = lax.broadcasted_iota(jnp.int32, (axes, hypos), 1)
    row_id = lax.broadcasted_iota(jnp.int32, (axes, LANES), 0)
    col_id = lax.broadcasted_iota(jnp.int32, (axes, LANES), 1)
    for t in range(temps):
        place = jnp.sum(
            jnp.where(h_id == hypo_ref[t], place_ref[...], 0.0), axis=1, keepdims=True
        )
        place_row = jnp.sum(jnp.where(row_id == col_id, place, 0.0), axis=0, keepdims=True)
        count_row = jnp.full((1, LANES), counts[t].astype(jnp.float32))
        for b in range(chunks):
            part_ref[b, t, pl.ds(0, share), :] = acc[t, pl.ds(b * share, share), :]
            part_ref[b, t, pl.ds(share, 1), :] = count_row
            part_ref[b, t, pl.ds(share + 1, 1), :] = place_row
            if chunk_rows > share + 2:
                part_ref[b, t, pl.ds(share + 2, chunk_rows - share - 2), :] = jnp.zeros(
                    (chunk_rows - share - 2, LANES), jnp.float32
                )

    pl.semaphore_wait(barrier, n_sta + n_tmpl - 2)
    copies = []
    for k in range(1, n_sta):
        peer = lax.rem(sta + k, n_sta)
        copies.append(
            pltpu.make_async_remote_copy(
                src_ref=part_ref.at[peer],
                dst_ref=held.at[k - 1],
                send_sem=send_a.at[k - 1],
                recv_sem=recv_a.at[k - 1],
                device_id={"sta": peer},
                device_id_type=pl.DeviceIdType.MESH,
            )
        )
        copies[-1].start()
    own = part_ref[sta]
    whole = own
    for k, copy in enumerate(copies):
        copy.wait_recv()
        whole = whole + held[k]
    row_id = lax.broadcasted_iota(jnp.int32, whole.shape, 1)
    out_ref[0] = jnp.where(
        row_id < share, sharpness * (whole / whole[:, share : share + 1, :]), own
    )
    later = []
    for k in range(1, n_tmpl):
        later.append(
            pltpu.make_async_remote_copy(
                src_ref=out_ref.at[0],
                dst_ref=out_ref.at[k],
                send_sem=send_b.at[k - 1],
                recv_sem=recv_b.at[k - 1],
                device_id={"tmpl": lax.rem(tmpl + k, n_tmpl)},
                device_id_type=pl.DeviceIdType.MESH,
            )
        )
        later[-1].start()
    for copy in copies:
        copy.wait_send()
    for copy in later:
        copy.wait()


def all_scores(records, templates, channel_valid, shifts, hypo_id, hypo_xyz):
    stations, comps, samples = records.shape
    temps, taps = templates.shape[0], templates.shape[-1]
    rows = samples // LANES
    prows = -(-(rows + 1) // 8) * 8
    total = stations * comps * prows
    group = math.gcd(stations, 16)
    unroll = math.gcd(stations, 2)
    n_sta, n_tmpl = lax.axis_size("sta"), lax.axis_size("tmpl")
    out_rows = SAMPLES // LANES
    chunk_rows = -(-(out_rows // n_sta + 2) // 8) * 8
    axes, hypos = hypo_xyz.shape
    block = (temps, chunk_rows, LANES)
    return pl.pallas_call(
        functools.partial(trace_kernel, taps, group, unroll, n_sta, n_tmpl),
        out_shape=jax.ShapeDtypeStruct((n_tmpl,) + block, jnp.float32),
        in_specs=[pl.BlockSpec(memory_space=pltpu.HBM)] * 6,
        out_specs=pl.BlockSpec(memory_space=pltpu.VMEM),
        scratch_shapes=[
            pltpu.SMEM((temps, stations), jnp.int32),
            pltpu.SMEM((comps, temps, stations), jnp.int32),
            pltpu.SMEM((temps,), jnp.int32),
            pltpu.VMEM((axes, hypos), jnp.float32),
            pltpu.VMEM((comps, stations, samples), jnp.bfloat16),
            pltpu.VMEM((temps, comps, stations, taps), jnp.bfloat16),
            pltpu.VMEM((total + 8, LANES), jnp.float32),
            pltpu.VMEM((total, 2 * LANES), jnp.bfloat16),
            pltpu.VMEM((total, LANES), jnp.float32),
            pltpu.VMEM((comps * temps * stations, LANES), jnp.float32),
            pltpu.VMEM((temps, out_rows, LANES), jnp.float32),
            pltpu.VMEM((unroll, temps, prows, LANES), jnp.float32),
            pltpu.VMEM((n_sta,) + block, jnp.float32),
            pltpu.VMEM((n_sta - 1,) + block, jnp.float32),
            pltpu.SemaphoreType.DMA((5,)),
            pltpu.SemaphoreType.DMA((stations // group,)),
            pltpu.SemaphoreType.DMA((n_sta - 1,)),
            pltpu.SemaphoreType.DMA((n_sta - 1,)),
            pltpu.SemaphoreType.DMA((n_tmpl - 1,)),
            pltpu.SemaphoreType.DMA((n_tmpl - 1,)),
        ],
        compiler_params=pltpu.CompilerParams(
            vmem_limit_bytes=60 * 2**20, collective_id=0, has_side_effects=True
        ),
        name="traces",
    )(
        shifts,
        jnp.transpose(channel_valid, (2, 0, 1)),
        hypo_id,
        hypo_xyz,
        jnp.transpose(records, (1, 0, 2)),
        jnp.transpose(templates, (0, 2, 1, 3)),
    )


def finish_kernel(
    share, axes, score_ref, best_hbm, evidence_hbm, place_hbm,
    best_ref, evidence_ref, place_ref, sem
):
    groups, temps = score_ref.shape[:2]
    pieces = [score_ref[n, t] for n in range(groups) for t in range(temps)]
    best = pieces[0]
    for piece in pieces[1:]:
        best = jnp.maximum(best, piece)
    best_ref[...] = best[:share]
    copies = [pltpu.make_async_copy(best_ref, best_hbm, sem.at[0])]
    copies[-1].start()
    total = jnp.zeros_like(best)
    sums = [jnp.zeros_like(best) for _ in range(axes)]
    for piece in pieces:
        weight = jnp.exp(piece - best)
        total = total + weight
        for j in range(axes):
            sums[j] = sums[j] + weight * piece[share + 1 : share + 2, j : j + 1]
    evidence_ref[...] = (best + jnp.log(total))[:share]
    copies.append(pltpu.make_async_copy(evidence_ref, evidence_hbm, sem.at[1]))
    copies[-1].start()
    for j in range(axes):
        located = sums[j] / total
        for r in range(share):
            place_ref[pl.ds(j, 1), pl.ds(r * LANES, LANES)] = located[r : r + 1]
    copies.append(pltpu.make_async_copy(place_ref, place_hbm, sem.at[2]))
    copies[-1].start()
    for copy in copies:
        copy.wait()


def on_device(records, templates, channel_valid, shifts, hypo_id, hypo_xyz):
    scores = all_scores(records, templates, channel_valid, shifts, hypo_id, hypo_xyz)
    axes = hypo_xyz.shape[0]
    share = SAMPLES // LANES // lax.axis_size("sta")
    hbm = pl.BlockSpec(memory_space=pltpu.HBM)
    shapes = ((share, LANES), (share, LANES), (axes, share * LANES))
    best, evidence, location = pl.pallas_call(
        functools.partial(finish_kernel, share, axes),
        out_shape=tuple(jax.ShapeDtypeStruct(shape, jnp.float32) for shape in shapes),
        in_specs=[pl.BlockSpec(memory_space=pltpu.VMEM)],
        out_specs=(hbm, hbm, hbm),
        scratch_shapes=[pltpu.VMEM(shape, jnp.float32) for shape in shapes]
        + [pltpu.SemaphoreType.DMA((3,))],
        name="finish",
    )(scores)
    return (best.reshape(-1), evidence.reshape(-1), location)


def solution(mesh):
    return jax.shard_map(
        on_device,
        mesh=mesh,
        in_specs=(
            P(("win", "sta"), None, None),
            P(("win", "tmpl"), "sta", None, None),
            P(("win", "tmpl"), "sta", None),
            P(("win", "tmpl"), "sta"),
            P(("win", "tmpl")),
            P(),
        ),
        out_specs=(P(("win", "sta")), P(("win", "sta")), P(None, ("win", "sta"))),
        check_vma=False,
    )
```

```python
import functools
import math

import jax
import jax.numpy as jnp
from jax import lax
from jax.experimental import pallas as pl
from jax.experimental.pallas import tpu as pltpu
from jax.sharding import PartitionSpec as P

SAMPLES = 3072

sharpness = 400.0
epsilon = 1e-06
LANES = 128
HALF = 64


def trace_kernel(
    taps, group, chans, unroll, n_sta, n_tmpl,
    shift_hbm, valid_hbm, hypo_hbm, place_hbm, x_hbm, w_hbm, out_ref,
    shift_ref, valid_ref, hypo_ref, place_ref, x_ref, w_ref,
    xs, xw, rn, ws, acc, scr, part_ref, held,
    sem_in, sem_x, send_a, recv_a, send_b, recv_b
):
    comps, stations, samples = x_ref.shape
    chunks, temps, chunk_rows = part_ref.shape[:3]
    sta, tmpl = lax.axis_index("sta"), lax.axis_index("tmpl")
    barrier = pltpu.get_barrier_semaphore()
    for axis, me, size in (("sta", sta, n_sta), ("tmpl", tmpl, n_tmpl)):
        for k in range(1, size):
            pl.semaphore_signal(
                barrier, inc=1, device_id={axis: lax.rem(me + k, size)},
                device_id_type=pl.DeviceIdType.MESH,
            )
    w_copy = pltpu.make_async_copy(w_hbm, w_ref, sem_in.at[0])
    w_copy.start()
    x_copies = []
    for g in range(stations // group):
        span = pl.ds(g * group, group)
        x_copies.append(
            pltpu.make_async_copy(x_hbm.at[:, span, :], x_ref.at[:, span, :], sem_x.at[g])
        )
        x_copies[-1].start()
    small = []
    for n, (src, dst) in enumerate(
        (
            (shift_hbm, shift_ref), (valid_hbm, valid_ref),
            (hypo_hbm, hypo_ref), (place_hbm, place_ref),
        )
    ):
        small.append(pltpu.make_async_copy(src, dst, sem_in.at[n + 1]))
        small[-1].start()
    out_rows = acc.shape[1]
    rows = samples // LANES
    prows = -(-(rows + 1) // 8) * 8
    srows = comps * prows
    j_id = lax.broadcasted_iota(jnp.int32, (LANES, LANES), 0)
    i_id = lax.broadcasted_iota(jnp.int32, (LANES, LANES), 1)
    gap = j_id - i_id
    band = jnp.concatenate(
        [
            jnp.where((gap >= 0) & (gap < taps), 1.0, 0.0),
            jnp.where(gap + LANES < taps, 1.0, 0.0),
        ],
        axis=0,
    ).astype(jnp.bfloat16)

    k_id = lax.broadcasted_iota(jnp.int32, (taps, LANES), 0)
    l_id = lax.broadcasted_iota(jnp.int32, (taps, LANES), 1)
    turns = [
        jnp.where(
            lax.bitwise_and(k_id + l_id - first, LANES - 1) == 0, 1.0, 0.0
        ).astype(jnp.bfloat16)
        for first in (0, HALF)
    ]
    w_copy.wait()
    for c in range(comps):
        for t in range(temps):
            wide = w_ref[t, c].astype(jnp.float32)
            power = jnp.sum(wide * wide, axis=-1, keepdims=True) / taps
            normed = (wide / (taps * jnp.sqrt(power + epsilon))).astype(jnp.bfloat16)
            ws[pl.ds((c * temps + t) * stations, stations), :] = jnp.dot(
                normed, turns[t % 2], preferred_element_type=jnp.float32
            )

    xs[pl.ds(stations * srows, 8), :] = jnp.zeros((8, LANES), jnp.float32)

    def spread(g):
        base = g * (group * srows)
        for k in range(group * comps):
            xs[pl.ds(base + k * prows + prows - 8, 8), :] = jnp.zeros((8, LANES), jnp.float32)
        for c in range(comps):
            wave = x_ref[c, pl.ds(g * group, group), :].astype(jnp.float32)
            for r in range(rows):
                xs[pl.ds(base + c * prows + r, group, stride=srows), :] = wave[
                    :, r * LANES : (r + 1) * LANES
                ]

    def prepare(g, _):
        base = pl.multiple_of(g * (chans * prows), 8)
        mine = pl.ds(g * chans, chans)
        here = xs[pl.ds(base, chans * prows), :]
        after = xs[pl.ds(base + 1, chans * prows), :]
        left = lax.broadcasted_iota(jnp.int32, here.shape, 1) < HALF
        here_half = pltpu.roll(here, HALF, 1)
        after_half = pltpu.roll(after, HALF, 1)
        window = jnp.concatenate([here, after], axis=1)
        middle = jnp.concatenate([jnp.where(left, here_half, after_half), after_half], axis=1)
        xw[mine, pl.ds(0, prows), :] = window.astype(jnp.bfloat16).reshape(chans, prows, -1)
        xw[mine, pl.ds(prows, prows), :] = middle.astype(jnp.bfloat16).reshape(chans, prows, -1)
        square = window * window
        high = square.astype(jnp.bfloat16)
        low = (square - high.astype(jnp.float32)).astype(jnp.bfloat16)
        energy = jnp.dot(high, band, preferred_element_type=jnp.float32) + jnp.dot(
            low, band, preferred_element_type=jnp.float32
        )
        inverse = lax.rsqrt(energy * (1.0 / taps) + epsilon)
        swapped = pltpu.roll(inverse, HALF, 1)
        rn[mine, pl.ds(0, prows), :] = jnp.where(left, inverse, swapped).reshape(
            chans, prows, LANES
        )
        rn[mine, pl.ds(prows, prows), :] = jnp.where(left, swapped, inverse).reshape(
            chans, prows, LANES
        )
        return 0

    for g, copy in enumerate(x_copies):
        copy.wait()
        spread(g)
    lax.fori_loop(0, stations * comps // chans, prepare, 0)
    for copy in small:
        copy.wait()

    lane = lax.broadcasted_iota(jnp.int32, (out_rows, LANES), 1)

    left = lax.broadcasted_iota(jnp.int32, (LANES, LANES), 1) < HALF
    step = lax.bitwise_and(i_id, HALF - 1)
    depth = -(-(taps + HALF - 1) // 16) * 16
    rest = depth - LANES

    def one_station(s, slot, counts):
        counts = list(counts)
        traces = []
        for pair in range(temps // 2):
            sums = None
            for c in range(comps):
                rings = []
                for t in (2 * pair, 2 * pair + 1):
                    valid = valid_ref[c, t, s]
                    counts[t] = counts[t] + valid
                    row = ws[pl.ds((c * temps + t) * stations + s, 1), :] * valid.astype(
                        jnp.float32
                    )
                    rings.append(
                        pltpu.roll(
                            jnp.broadcast_to(row, (LANES, LANES)), 0, 1, stride=1, stride_axis=0
                        )
                    )
                ring = jnp.where(left, rings[0], rings[1])
                tile = jnp.concatenate(
                    [
                        jnp.where(j_id[:HALF] >= step[:HALF], ring[:HALF], 0.0),
                        ring[HALF:],
                        jnp.where(j_id[:rest] < step[:rest], ring[:rest], 0.0),
                    ],
                    axis=0,
                ).astype(jnp.bfloat16)
                raw = jnp.dot(
                    xw[s * comps + c][:, :depth], tile, preferred_element_type=jnp.float32
                )
                term = raw * rn[s * comps + c]
                sums = term if sums is None else sums + term
            low, high = sums[:prows], sums[prows:]
            near = left[:prows]
            traces.append(jnp.where(near, low, pltpu.roll(high, HALF, 1)))
            traces.append(jnp.where(near, pltpu.roll(low, HALF, 1), high))
        for t in range(temps):
            shift = shift_ref[t, s]
            whole = lax.shift_right_logical(shift, 7)
            part = lax.bitwise_and(shift, LANES - 1)
            scr[slot, t] = pltpu.roll(
                traces[t], lax.bitwise_and(LANES - part, LANES - 1), 1
            )
            near = scr[slot, t, pl.ds(whole, out_rows), :]
            far = scr[slot, t, pl.ds(whole + 1, out_rows), :]
            acc[t] += jnp.where(lane < LANES - part, near, far)
        return tuple(counts)

    acc[...] = jnp.zeros_like(acc)

    def some_stations(g, counts):
        for k in range(unroll):
            counts = one_station(g * unroll + k, k, counts)
        return counts

    counts = lax.fori_loop(
        0, stations // unroll, some_stations, tuple(jnp.int32(0) for _ in range(temps))
    )

    share = out_rows // chunks
    axes, hypos = place_ref.shape
    h_id = lax.broadcasted_iota(jnp.int32, (axes, hypos), 1)
    row_id = lax.broadcasted_iota(jnp.int32, (axes, LANES), 0)
    col_id = lax.broadcasted_iota(jnp.int32, (axes, LANES), 1)
    for t in range(temps):
        place = jnp.sum(
            jnp.where(h_id == hypo_ref[t], place_ref[...], 0.0), axis=1, keepdims=True
        )
        place_row = jnp.sum(jnp.where(row_id == col_id, place, 0.0), axis=0, keepdims=True)
        count_row = jnp.full((1, LANES), counts[t].astype(jnp.float32))
        for b in range(chunks):
            part_ref[b, t, pl.ds(0, share), :] = acc[t, pl.ds(b * share, share), :]
            part_ref[b, t, pl.ds(share, 1), :] = count_row
            part_ref[b, t, pl.ds(share + 1, 1), :] = place_row
            if chunk_rows > share + 2:
                part_ref[b, t, pl.ds(share + 2, chunk_rows - share - 2), :] = jnp.zeros(
                    (chunk_rows - share - 2, LANES), jnp.float32
                )

    pl.semaphore_wait(barrier, n_sta + n_tmpl - 2)
    copies = []
    for k in range(1, n_sta):
        peer = lax.rem(sta + k, n_sta)
        copies.append(
            pltpu.make_async_remote_copy(
                src_ref=part_ref.at[peer],
                dst_ref=held.at[k - 1],
                send_sem=send_a.at[k - 1],
                recv_sem=recv_a.at[k - 1],
                device_id={"sta": peer},
                device_id_type=pl.DeviceIdType.MESH,
            )
        )
        copies[-1].start()
    own = part_ref[sta]
    whole = own
    for k, copy in enumerate(copies):
        copy.wait_recv()
        whole = whole + held[k]
    row_id = lax.broadcasted_iota(jnp.int32, whole.shape, 1)
    out_ref[0] = jnp.where(
        row_id < share, sharpness * (whole / whole[:, share : share + 1, :]), own
    )
    later = []
    for k in range(1, n_tmpl):
        later.append(
            pltpu.make_async_remote_copy(
                src_ref=out_ref.at[0],
                dst_ref=out_ref.at[k],
                send_sem=send_b.at[k - 1],
                recv_sem=recv_b.at[k - 1],
                device_id={"tmpl": lax.rem(tmpl + k, n_tmpl)},
                device_id_type=pl.DeviceIdType.MESH,
            )
        )
        later[-1].start()
    for copy in copies:
        copy.wait_send()
    for copy in later:
        copy.wait()


def all_scores(records, templates, channel_valid, shifts, hypo_id, hypo_xyz):
    stations, comps, samples = records.shape
    temps, taps = templates.shape[0], templates.shape[-1]
    rows = samples // LANES
    prows = -(-(rows + 1) // 8) * 8
    total = stations * comps * prows
    group = math.gcd(stations, 16)
    chans = math.gcd(stations, 4) * comps
    unroll = math.gcd(stations, 2)
    assert temps % 2 == 0 and LANES - HALF + 1 < taps < LANES
    n_sta, n_tmpl = lax.axis_size("sta"), lax.axis_size("tmpl")
    out_rows = SAMPLES // LANES
    chunk_rows = -(-(out_rows // n_sta + 2) // 8) * 8
    axes, hypos = hypo_xyz.shape
    block = (temps, chunk_rows, LANES)
    return pl.pallas_call(
        functools.partial(trace_kernel, taps, group, chans, unroll, n_sta, n_tmpl),
        out_shape=jax.ShapeDtypeStruct((n_tmpl,) + block, jnp.float32),
        in_specs=[pl.BlockSpec(memory_space=pltpu.HBM)] * 6,
        out_specs=pl.BlockSpec(memory_space=pltpu.VMEM),
        scratch_shapes=[
            pltpu.SMEM((temps, stations), jnp.int32),
            pltpu.SMEM((comps, temps, stations), jnp.int32),
            pltpu.SMEM((temps,), jnp.int32),
            pltpu.VMEM((axes, hypos), jnp.float32),
            pltpu.VMEM((comps, stations, samples), jnp.bfloat16),
            pltpu.VMEM((temps, comps, stations, taps), jnp.bfloat16),
            pltpu.VMEM((total + 8, LANES), jnp.float32),
            pltpu.VMEM((stations * comps, 2 * prows, 2 * LANES), jnp.bfloat16),
            pltpu.VMEM((stations * comps, 2 * prows, LANES), jnp.float32),
            pltpu.VMEM((comps * temps * stations, LANES), jnp.float32),
            pltpu.VMEM((temps, out_rows, LANES), jnp.float32),
            pltpu.VMEM((unroll, temps, prows, LANES), jnp.float32),
            pltpu.VMEM((n_sta,) + block, jnp.float32),
            pltpu.VMEM((n_sta - 1,) + block, jnp.float32),
            pltpu.SemaphoreType.DMA((5,)),
            pltpu.SemaphoreType.DMA((stations // group,)),
            pltpu.SemaphoreType.DMA((n_sta - 1,)),
            pltpu.SemaphoreType.DMA((n_sta - 1,)),
            pltpu.SemaphoreType.DMA((n_tmpl - 1,)),
            pltpu.SemaphoreType.DMA((n_tmpl - 1,)),
        ],
        compiler_params=pltpu.CompilerParams(
            vmem_limit_bytes=60 * 2**20, collective_id=0, has_side_effects=True
        ),
        name="traces",
    )(
        shifts,
        jnp.transpose(channel_valid, (2, 0, 1)),
        hypo_id,
        hypo_xyz,
        jnp.transpose(records, (1, 0, 2)),
        jnp.transpose(templates, (0, 2, 1, 3)),
    )


def finish_kernel(
    share, axes, score_ref, best_hbm, evidence_hbm, place_hbm,
    best_ref, evidence_ref, place_ref, sem
):
    groups, temps = score_ref.shape[:2]
    pieces = [score_ref[n, t] for n in range(groups) for t in range(temps)]
    best = pieces[0]
    for piece in pieces[1:]:
        best = jnp.maximum(best, piece)
    best_ref[...] = best[:share]
    copies = [pltpu.make_async_copy(best_ref, best_hbm, sem.at[0])]
    copies[-1].start()
    total = jnp.zeros_like(best)
    sums = [jnp.zeros_like(best) for _ in range(axes)]
    for piece in pieces:
        weight = jnp.exp(piece - best)
        total = total + weight
        for j in range(axes):
            sums[j] = sums[j] + weight * piece[share + 1 : share + 2, j : j + 1]
    evidence_ref[...] = (best + jnp.log(total))[:share]
    copies.append(pltpu.make_async_copy(evidence_ref, evidence_hbm, sem.at[1]))
    copies[-1].start()
    for j in range(axes):
        located = sums[j] / total
        for r in range(share):
            place_ref[pl.ds(j, 1), pl.ds(r * LANES, LANES)] = located[r : r + 1]
    copies.append(pltpu.make_async_copy(place_ref, place_hbm, sem.at[2]))
    copies[-1].start()
    for copy in copies:
        copy.wait()


def on_device(records, templates, channel_valid, shifts, hypo_id, hypo_xyz):
    scores = all_scores(records, templates, channel_valid, shifts, hypo_id, hypo_xyz)
    axes = hypo_xyz.shape[0]
    share = SAMPLES // LANES // lax.axis_size("sta")
    hbm = pl.BlockSpec(memory_space=pltpu.HBM)
    shapes = ((share, LANES), (share, LANES), (axes, share * LANES))
    best, evidence, location = pl.pallas_call(
        functools.partial(finish_kernel, share, axes),
        out_shape=tuple(jax.ShapeDtypeStruct(shape, jnp.float32) for shape in shapes),
        in_specs=[pl.BlockSpec(memory_space=pltpu.VMEM)],
        out_specs=(hbm, hbm, hbm),
        scratch_shapes=[pltpu.VMEM(shape, jnp.float32) for shape in shapes]
        + [pltpu.SemaphoreType.DMA((3,))],
        name="finish",
    )(scores)
    return (best.reshape(-1), evidence.reshape(-1), location)


def solution(mesh):
    return jax.shard_map(
        on_device,
        mesh=mesh,
        in_specs=(
            P(("win", "sta"), None, None),
            P(("win", "tmpl"), "sta", None, None),
            P(("win", "tmpl"), "sta", None),
            P(("win", "tmpl"), "sta"),
            P(("win", "tmpl")),
            P(),
        ),
        out_specs=(P(("win", "sta")), P(("win", "sta")), P(None, ("win", "sta"))),
        check_vma=False,
    )
```

```python
import functools
import math

import jax
import jax.numpy as jnp
from jax import lax
from jax.experimental import pallas as pl
from jax.experimental.pallas import tpu as pltpu
from jax.sharding import PartitionSpec as P

SAMPLES = 3072

sharpness = 400.0
epsilon = 1e-06
LANES = 128


def trace_kernel(
    taps, group, unroll, n_sta, n_tmpl,
    shift_hbm, valid_hbm, hypo_hbm, place_hbm, x_hbm, w_hbm, out_ref,
    shift_ref, valid_ref, hypo_ref, place_ref, x_ref, w_ref,
    xs, xw, rn, ws, acc, scr, part_ref, held,
    sem_in, sem_x, send_a, recv_a, send_b, recv_b
):
    comps, stations, samples = x_ref.shape
    chunks, temps, chunk_rows = part_ref.shape[:3]
    sta, tmpl = lax.axis_index("sta"), lax.axis_index("tmpl")
    barrier = pltpu.get_barrier_semaphore()
    for axis, me, size in (("sta", sta, n_sta), ("tmpl", tmpl, n_tmpl)):
        for k in range(1, size):
            pl.semaphore_signal(
                barrier, inc=1, device_id={axis: lax.rem(me + k, size)},
                device_id_type=pl.DeviceIdType.MESH,
            )
    w_copy = pltpu.make_async_copy(w_hbm, w_ref, sem_in.at[0])
    w_copy.start()
    x_copies = []
    for g in range(stations // group):
        span = pl.ds(g * group, group)
        x_copies.append(
            pltpu.make_async_copy(x_hbm.at[:, span, :], x_ref.at[:, span, :], sem_x.at[g])
        )
        x_copies[-1].start()
    small = []
    for n, (src, dst) in enumerate(
        (
            (shift_hbm, shift_ref), (valid_hbm, valid_ref),
            (hypo_hbm, hypo_ref), (place_hbm, place_ref),
        )
    ):
        small.append(pltpu.make_async_copy(src, dst, sem_in.at[n + 1]))
        small[-1].start()
    out_rows = acc.shape[1]
    rows = samples // LANES
    prows = -(-(rows + 1) // 8) * 8
    srows = comps * prows
    j_id = lax.broadcasted_iota(jnp.int32, (LANES, LANES), 0)
    i_id = lax.broadcasted_iota(jnp.int32, (LANES, LANES), 1)
    upper = j_id >= i_id
    gap = j_id - i_id
    band = jnp.concatenate(
        [
            jnp.where((gap >= 0) & (gap < taps), 1.0, 0.0),
            jnp.where(gap + LANES < taps, 1.0, 0.0),
        ],
        axis=0,
    ).astype(jnp.bfloat16)

    k_id = lax.broadcasted_iota(jnp.int32, (taps, LANES), 0)
    l_id = lax.broadcasted_iota(jnp.int32, (taps, LANES), 1)
    turn = jnp.where(lax.bitwise_and(k_id + l_id, LANES - 1) == 0, 1.0, 0.0).astype(jnp.bfloat16)
    w_copy.wait()
    for c in range(comps):
        for t in range(temps):
            wide = w_ref[t, c].astype(jnp.float32)
            power = jnp.sum(wide * wide, axis=-1, keepdims=True) / taps
            normed = (wide / (taps * jnp.sqrt(power + epsilon))).astype(jnp.bfloat16)
            ws[pl.ds((c * temps + t) * stations, stations), :] = jnp.dot(
                normed, turn, preferred_element_type=jnp.float32
            )

    xs[pl.ds(stations * srows, 8), :] = jnp.zeros((8, LANES), jnp.float32)

    def prepare(g, _):
        base = g * (group * srows)
        first = g * group
        for k in range(group * comps):
            xs[pl.ds(base + k * prows + prows - 8, 8), :] = jnp.zeros((8, LANES), jnp.float32)
        for c in range(comps):
            wave = x_ref[c, pl.ds(first, group), :].astype(jnp.float32)
            for r in range(rows):
                xs[pl.ds(base + c * prows + r, group, stride=srows), :] = wave[
                    :, r * LANES : (r + 1) * LANES
                ]
        count = group * srows
        here = xs[pl.ds(base, count), :]
        after = xs[pl.ds(base + 1, count), :]
        window = jnp.concatenate([here, after], axis=1)
        xw[pl.ds(base, count), :] = window.astype(jnp.bfloat16)
        square = window * window
        high = square.astype(jnp.bfloat16)
        low = (square - high.astype(jnp.float32)).astype(jnp.bfloat16)
        energy = jnp.dot(high, band, preferred_element_type=jnp.float32) + jnp.dot(
            low, band, preferred_element_type=jnp.float32
        )
        rn[pl.ds(base, count), :] = lax.rsqrt(energy * (1.0 / taps) + epsilon)
        return 0

    for g, copy in enumerate(x_copies):
        copy.wait()
        prepare(g, 0)
    for copy in small:
        copy.wait()

    lane = lax.broadcasted_iota(jnp.int32, (out_rows, LANES), 1)

    def one_station(s, slot, counts, moved):
        sums = [None] * temps
        counts, moved = list(counts), list(moved)
        for c in range(comps):
            base = pl.multiple_of((s * comps + c) * prows, 16)
            data = xw[pl.ds(base, prows), :]
            inverse = rn[pl.ds(base, prows), :]
            tiles = []
            for t in range(temps):
                valid = valid_ref[c, t, s]
                counts[t] = counts[t] + valid
                row = ws[pl.ds((c * temps + t) * stations + s, 1), :] * valid.astype(jnp.float32)
                ring = pltpu.roll(
                    jnp.broadcast_to(row, (LANES, LANES)), 0, 1, stride=1, stride_axis=0
                )
                tiles.append(
                    jnp.concatenate(
                        [jnp.where(upper, ring, 0.0), jnp.where(upper, 0.0, ring)], axis=0
                    ).astype(jnp.bfloat16)
                )
            raw = jnp.dot(
                data, jnp.concatenate(tiles, axis=1), preferred_element_type=jnp.float32
            )
            for t in range(temps):
                term = raw[:, t * LANES : (t + 1) * LANES] * inverse
                sums[t] = term if sums[t] is None else sums[t] + term
        for t in range(temps):
            shift = shift_ref[t, s]
            whole = lax.shift_right_logical(shift, 7)
            part = lax.bitwise_and(shift, LANES - 1)
            scr[slot, t] = pltpu.roll(
                sums[t], lax.bitwise_and(LANES - part, LANES - 1), 1
            )
            near = scr[slot, t, pl.ds(whole, out_rows), :]
            far = scr[slot, t, pl.ds(whole + 1, out_rows), :]
            moved[t] = moved[t] + jnp.where(lane < LANES - part, near, far)
        return counts, moved

    acc[...] = jnp.zeros_like(acc)

    def some_stations(g, counts):
        moved = [acc[t] for t in range(temps)]
        for k in range(unroll):
            counts, moved = one_station(g * unroll + k, k, counts, moved)
        for t in range(temps):
            acc[t] = moved[t]
        return tuple(counts)

    counts = lax.fori_loop(
        0, stations // unroll, some_stations, tuple(jnp.int32(0) for _ in range(temps))
    )

    share = out_rows // chunks
    axes, hypos = place_ref.shape
    h_id = lax.broadcasted_iota(jnp.int32, (axes, hypos), 1)
    row_id = lax.broadcasted_iota(jnp.int32, (axes, LANES), 0)
    col_id = lax.broadcasted_iota(jnp.int32, (axes, LANES), 1)
    for t in range(temps):
        place = jnp.sum(
            jnp.where(h_id == hypo_ref[t], place_ref[...], 0.0), axis=1, keepdims=True
        )
        place_row = jnp.sum(jnp.where(row_id == col_id, place, 0.0), axis=0, keepdims=True)
        count_row = jnp.full((1, LANES), counts[t].astype(jnp.float32))
        for b in range(chunks):
            part_ref[b, t, pl.ds(0, share), :] = acc[t, pl.ds(b * share, share), :]
            part_ref[b, t, pl.ds(share, 1), :] = count_row
            part_ref[b, t, pl.ds(share + 1, 1), :] = place_row
            if chunk_rows > share + 2:
                part_ref[b, t, pl.ds(share + 2, chunk_rows - share - 2), :] = jnp.zeros(
                    (chunk_rows - share - 2, LANES), jnp.float32
                )

    pl.semaphore_wait(barrier, n_sta + n_tmpl - 2)
    copies = []
    for k in range(1, n_sta):
        peer = lax.rem(sta + k, n_sta)
        copies.append(
            pltpu.make_async_remote_copy(
                src_ref=part_ref.at[peer],
                dst_ref=held.at[k - 1],
                send_sem=send_a.at[k - 1],
                recv_sem=recv_a.at[k - 1],
                device_id={"sta": peer},
                device_id_type=pl.DeviceIdType.MESH,
            )
        )
        copies[-1].start()
    own = part_ref[sta]
    whole = own
    for k, copy in enumerate(copies):
        copy.wait_recv()
        whole = whole + held[k]
    row_id = lax.broadcasted_iota(jnp.int32, whole.shape, 1)
    out_ref[0] = jnp.where(
        row_id < share, sharpness * (whole / whole[:, share : share + 1, :]), own
    )
    later = []
    for k in range(1, n_tmpl):
        later.append(
            pltpu.make_async_remote_copy(
                src_ref=out_ref.at[0],
                dst_ref=out_ref.at[k],
                send_sem=send_b.at[k - 1],
                recv_sem=recv_b.at[k - 1],
                device_id={"tmpl": lax.rem(tmpl + k, n_tmpl)},
                device_id_type=pl.DeviceIdType.MESH,
            )
        )
        later[-1].start()
    for copy in copies:
        copy.wait_send()
    for copy in later:
        copy.wait()


def all_scores(records, templates, channel_valid, shifts, hypo_id, hypo_xyz):
    stations, comps, samples = records.shape
    temps, taps = templates.shape[0], templates.shape[-1]
    rows = samples // LANES
    prows = -(-(rows + 1) // 8) * 8
    total = stations * comps * prows
    group = math.gcd(stations, 16)
    unroll = math.gcd(stations, 6)
    n_sta, n_tmpl = lax.axis_size("sta"), lax.axis_size("tmpl")
    out_rows = SAMPLES // LANES
    chunk_rows = -(-(out_rows // n_sta + 2) // 8) * 8
    axes, hypos = hypo_xyz.shape
    block = (temps, chunk_rows, LANES)
    return pl.pallas_call(
        functools.partial(trace_kernel, taps, group, unroll, n_sta, n_tmpl),
        out_shape=jax.ShapeDtypeStruct((n_tmpl,) + block, jnp.float32),
        in_specs=[pl.BlockSpec(memory_space=pltpu.HBM)] * 6,
        out_specs=pl.BlockSpec(memory_space=pltpu.VMEM),
        scratch_shapes=[
            pltpu.SMEM((temps, stations), jnp.int32),
            pltpu.SMEM((comps, temps, stations), jnp.int32),
            pltpu.SMEM((temps,), jnp.int32),
            pltpu.VMEM((axes, hypos), jnp.float32),
            pltpu.VMEM((comps, stations, samples), jnp.bfloat16),
            pltpu.VMEM((temps, comps, stations, taps), jnp.bfloat16),
            pltpu.VMEM((total + 8, LANES), jnp.float32),
            pltpu.VMEM((total, 2 * LANES), jnp.bfloat16),
            pltpu.VMEM((total, LANES), jnp.float32),
            pltpu.VMEM((comps * temps * stations, LANES), jnp.float32),
            pltpu.VMEM((temps, out_rows, LANES), jnp.float32),
            pltpu.VMEM((unroll, temps, prows, LANES), jnp.float32),
            pltpu.VMEM((n_sta,) + block, jnp.float32),
            pltpu.VMEM((n_sta - 1,) + block, jnp.float32),
            pltpu.SemaphoreType.DMA((5,)),
            pltpu.SemaphoreType.DMA((stations // group,)),
            pltpu.SemaphoreType.DMA((n_sta - 1,)),
            pltpu.SemaphoreType.DMA((n_sta - 1,)),
            pltpu.SemaphoreType.DMA((n_tmpl - 1,)),
            pltpu.SemaphoreType.DMA((n_tmpl - 1,)),
        ],
        compiler_params=pltpu.CompilerParams(
            vmem_limit_bytes=60 * 2**20, collective_id=0, has_side_effects=True
        ),
        name="traces",
    )(
        shifts,
        jnp.transpose(channel_valid, (2, 0, 1)),
        hypo_id,
        hypo_xyz,
        jnp.transpose(records, (1, 0, 2)),
        jnp.transpose(templates, (0, 2, 1, 3)),
    )


def finish_kernel(
    share, axes, score_ref, best_hbm, evidence_hbm, place_hbm,
    best_ref, evidence_ref, place_ref, sem
):
    groups, temps = score_ref.shape[:2]
    pieces = [score_ref[n, t] for n in range(groups) for t in range(temps)]
    best = pieces[0]
    for piece in pieces[1:]:
        best = jnp.maximum(best, piece)
    best_ref[...] = best[:share]
    copies = [pltpu.make_async_copy(best_ref, best_hbm, sem.at[0])]
    copies[-1].start()
    total = jnp.zeros_like(best)
    sums = [jnp.zeros_like(best) for _ in range(axes)]
    for piece in pieces:
        weight = jnp.exp(piece - best)
        total = total + weight
        for j in range(axes):
            sums[j] = sums[j] + weight * piece[share + 1 : share + 2, j : j + 1]
    evidence_ref[...] = (best + jnp.log(total))[:share]
    copies.append(pltpu.make_async_copy(evidence_ref, evidence_hbm, sem.at[1]))
    copies[-1].start()
    for j in range(axes):
        located = sums[j] / total
        for r in range(share):
            place_ref[pl.ds(j, 1), pl.ds(r * LANES, LANES)] = located[r : r + 1]
    copies.append(pltpu.make_async_copy(place_ref, place_hbm, sem.at[2]))
    copies[-1].start()
    for copy in copies:
        copy.wait()


def on_device(records, templates, channel_valid, shifts, hypo_id, hypo_xyz):
    scores = all_scores(records, templates, channel_valid, shifts, hypo_id, hypo_xyz)
    axes = hypo_xyz.shape[0]
    share = SAMPLES // LANES // lax.axis_size("sta")
    hbm = pl.BlockSpec(memory_space=pltpu.HBM)
    shapes = ((share, LANES), (share, LANES), (axes, share * LANES))
    best, evidence, location = pl.pallas_call(
        functools.partial(finish_kernel, share, axes),
        out_shape=tuple(jax.ShapeDtypeStruct(shape, jnp.float32) for shape in shapes),
        in_specs=[pl.BlockSpec(memory_space=pltpu.VMEM)],
        out_specs=(hbm, hbm, hbm),
        scratch_shapes=[pltpu.VMEM(shape, jnp.float32) for shape in shapes]
        + [pltpu.SemaphoreType.DMA((3,))],
        name="finish",
    )(scores)
    return (best.reshape(-1), evidence.reshape(-1), location)


def solution(mesh):
    return jax.shard_map(
        on_device,
        mesh=mesh,
        in_specs=(
            P(("win", "sta"), None, None),
            P(("win", "tmpl"), "sta", None, None),
            P(("win", "tmpl"), "sta", None),
            P(("win", "tmpl"), "sta"),
            P(("win", "tmpl")),
            P(),
        ),
        out_specs=(P(("win", "sta")), P(("win", "sta")), P(None, ("win", "sta"))),
        check_vma=False,
    )
```

```python
import functools
import math

import jax
import jax.numpy as jnp
from jax import lax
from jax.experimental import pallas as pl
from jax.experimental.pallas import tpu as pltpu
from jax.sharding import PartitionSpec as P

SAMPLES = 3072

sharpness = 400.0
epsilon = 1e-06
LANES = 128
HALF = 64


def trace_kernel(
    taps, group, chans, unroll, n_sta, n_tmpl,
    shift_hbm, valid_hbm, hypo_hbm, place_hbm, x_hbm, w_hbm, out_ref,
    shift_ref, valid_ref, hypo_ref, place_ref, x_ref, w_ref,
    xs, xw, rn, ws, acc, scr, part_ref, held,
    sem_in, sem_x, send_a, recv_a, send_b, recv_b
):
    comps, stations, samples = x_ref.shape
    chunks, temps, chunk_rows = part_ref.shape[:3]
    sta, tmpl = lax.axis_index("sta"), lax.axis_index("tmpl")
    barrier = pltpu.get_barrier_semaphore()
    for axis, me, size in (("sta", sta, n_sta), ("tmpl", tmpl, n_tmpl)):
        for k in range(1, size):
            pl.semaphore_signal(
                barrier, inc=1, device_id={axis: lax.rem(me + k, size)},
                device_id_type=pl.DeviceIdType.MESH,
            )
    w_copy = pltpu.make_async_copy(w_hbm, w_ref, sem_in.at[0])
    w_copy.start()
    x_copies = []
    for g in range(stations // group):
        span = pl.ds(g * group, group)
        x_copies.append(
            pltpu.make_async_copy(x_hbm.at[:, span, :], x_ref.at[:, span, :], sem_x.at[g])
        )
        x_copies[-1].start()
    small = []
    for n, (src, dst) in enumerate(
        (
            (shift_hbm, shift_ref), (valid_hbm, valid_ref),
            (hypo_hbm, hypo_ref), (place_hbm, place_ref),
        )
    ):
        small.append(pltpu.make_async_copy(src, dst, sem_in.at[n + 1]))
        small[-1].start()
    out_rows = acc.shape[1]
    rows = samples // LANES
    prows = -(-(rows + 1) // 8) * 8
    srows = comps * prows
    j_id = lax.broadcasted_iota(jnp.int32, (LANES, LANES), 0)
    i_id = lax.broadcasted_iota(jnp.int32, (LANES, LANES), 1)
    gap = j_id - i_id
    band = jnp.concatenate(
        [
            jnp.where((gap >= 0) & (gap < taps), 1.0, 0.0),
            jnp.where(gap + LANES < taps, 1.0, 0.0),
        ],
        axis=0,
    ).astype(jnp.bfloat16)

    k_id = lax.broadcasted_iota(jnp.int32, (taps, LANES), 0)
    l_id = lax.broadcasted_iota(jnp.int32, (taps, LANES), 1)
    turns = [
        jnp.where(
            lax.bitwise_and(k_id + l_id - first, LANES - 1) == 0, 1.0, 0.0
        ).astype(jnp.bfloat16)
        for first in (0, HALF)
    ]
    w_copy.wait()
    for c in range(comps):
        for t in range(temps):
            wide = w_ref[t, c].astype(jnp.float32)
            power = jnp.sum(wide * wide, axis=-1, keepdims=True) / taps
            normed = (wide / (taps * jnp.sqrt(power + epsilon))).astype(jnp.bfloat16)
            ws[pl.ds((c * temps + t) * stations, stations), :] = jnp.dot(
                normed, turns[t % 2], preferred_element_type=jnp.float32
            )

    xs[pl.ds(stations * srows, 8), :] = jnp.zeros((8, LANES), jnp.float32)

    def spread(g):
        base = g * (group * srows)
        for k in range(group * comps):
            xs[pl.ds(base + k * prows + prows - 8, 8), :] = jnp.zeros((8, LANES), jnp.float32)
        for c in range(comps):
            wave = x_ref[c, pl.ds(g * group, group), :].astype(jnp.float32)
            for r in range(rows):
                xs[pl.ds(base + c * prows + r, group, stride=srows), :] = wave[
                    :, r * LANES : (r + 1) * LANES
                ]

    def prepare(g, _):
        base = g * (chans * prows)
        mine = pl.ds(g * chans, chans)
        here = xs[pl.ds(base, chans * prows), :]
        after = xs[pl.ds(base + 1, chans * prows), :]
        left = lax.broadcasted_iota(jnp.int32, here.shape, 1) < HALF
        here_half = pltpu.roll(here, HALF, 1)
        after_half = pltpu.roll(after, HALF, 1)
        window = jnp.concatenate([here, after], axis=1)
        middle = jnp.concatenate([jnp.where(left, here_half, after_half), after_half], axis=1)
        xw[mine, pl.ds(0, prows), :] = window.astype(jnp.bfloat16).reshape(chans, prows, -1)
        xw[mine, pl.ds(prows, prows), :] = middle.astype(jnp.bfloat16).reshape(chans, prows, -1)
        square = window * window
        high = square.astype(jnp.bfloat16)
        low = (square - high.astype(jnp.float32)).astype(jnp.bfloat16)
        energy = jnp.dot(high, band, preferred_element_type=jnp.float32) + jnp.dot(
            low, band, preferred_element_type=jnp.float32
        )
        inverse = lax.rsqrt(energy * (1.0 / taps) + epsilon)
        swapped = pltpu.roll(inverse, HALF, 1)
        rn[mine, pl.ds(0, prows), :] = jnp.where(left, inverse, swapped).reshape(
            chans, prows, LANES
        )
        rn[mine, pl.ds(prows, prows), :] = jnp.where(left, swapped, inverse).reshape(
            chans, prows, LANES
        )
        return 0

    for g, copy in enumerate(x_copies):
        copy.wait()
        spread(g)
        prepare(g, 0)
    for copy in small:
        copy.wait()

    lane = lax.broadcasted_iota(jnp.int32, (out_rows, LANES), 1)

    left = lax.broadcasted_iota(jnp.int32, (LANES, LANES), 1) < HALF
    step = lax.bitwise_and(i_id, HALF - 1)
    depth = -(-(taps + HALF - 1) // 16) * 16
    rest = depth - LANES

    def one_station(s, slot, counts, moved):
        counts, moved = list(counts), list(moved)
        traces = []
        for pair in range(temps // 2):
            sums = None
            for c in range(comps):
                rings = []
                for t in (2 * pair, 2 * pair + 1):
                    valid = valid_ref[c, t, s]
                    counts[t] = counts[t] + valid
                    row = ws[pl.ds((c * temps + t) * stations + s, 1), :] * valid.astype(
                        jnp.float32
                    )
                    rings.append(
                        pltpu.roll(
                            jnp.broadcast_to(row, (LANES, LANES)), 0, 1, stride=1, stride_axis=0
                        )
                    )
                ring = jnp.where(left, rings[0], rings[1])
                tile = jnp.concatenate(
                    [
                        jnp.where(j_id[:HALF] >= step[:HALF], ring[:HALF], 0.0),
                        ring[HALF:],
                        jnp.where(j_id[:rest] < step[:rest], ring[:rest], 0.0),
                    ],
                    axis=0,
                ).astype(jnp.bfloat16)
                raw = jnp.dot(
                    xw[s * comps + c][:, :depth], tile, preferred_element_type=jnp.float32
                )
                term = raw * rn[s * comps + c]
                sums = term if sums is None else sums + term
            low, high = sums[:prows], sums[prows:]
            near = left[:prows]
            traces.append(jnp.where(near, low, pltpu.roll(high, HALF, 1)))
            traces.append(jnp.where(near, pltpu.roll(low, HALF, 1), high))
        for t in range(temps):
            shift = shift_ref[t, s]
            whole = lax.shift_right_logical(shift, 7)
            part = lax.bitwise_and(shift, LANES - 1)
            scr[slot, t] = pltpu.roll(
                traces[t], lax.bitwise_and(LANES - part, LANES - 1), 1
            )
            near = scr[slot, t, pl.ds(whole, out_rows), :]
            far = scr[slot, t, pl.ds(whole + 1, out_rows), :]
            moved[t] = moved[t] + jnp.where(lane < LANES - part, near, far)
        return counts, moved

    acc[...] = jnp.zeros_like(acc)

    def some_stations(g, counts):
        moved = [acc[t] for t in range(temps)]
        for k in range(unroll):
            counts, moved = one_station(g * unroll + k, k, counts, moved)
        for t in range(temps):
            acc[t] = moved[t]
        return tuple(counts)

    counts = lax.fori_loop(
        0, stations // unroll, some_stations, tuple(jnp.int32(0) for _ in range(temps))
    )

    share = out_rows // chunks
    axes, hypos = place_ref.shape
    h_id = lax.broadcasted_iota(jnp.int32, (axes, hypos), 1)
    row_id = lax.broadcasted_iota(jnp.int32, (axes, LANES), 0)
    col_id = lax.broadcasted_iota(jnp.int32, (axes, LANES), 1)
    for t in range(temps):
        place = jnp.sum(
            jnp.where(h_id == hypo_ref[t], place_ref[...], 0.0), axis=1, keepdims=True
        )
        place_row = jnp.sum(jnp.where(row_id == col_id, place, 0.0), axis=0, keepdims=True)
        count_row = jnp.full((1, LANES), counts[t].astype(jnp.float32))
        for b in range(chunks):
            part_ref[b, t, pl.ds(0, share), :] = acc[t, pl.ds(b * share, share), :]
            part_ref[b, t, pl.ds(share, 1), :] = count_row
            part_ref[b, t, pl.ds(share + 1, 1), :] = place_row
            if chunk_rows > share + 2:
                part_ref[b, t, pl.ds(share + 2, chunk_rows - share - 2), :] = jnp.zeros(
                    (chunk_rows - share - 2, LANES), jnp.float32
                )

    pl.semaphore_wait(barrier, n_sta + n_tmpl - 2)
    copies = []
    for k in range(1, n_sta):
        peer = lax.rem(sta + k, n_sta)
        copies.append(
            pltpu.make_async_remote_copy(
                src_ref=part_ref.at[peer],
                dst_ref=held.at[k - 1],
                send_sem=send_a.at[k - 1],
                recv_sem=recv_a.at[k - 1],
                device_id={"sta": peer},
                device_id_type=pl.DeviceIdType.MESH,
            )
        )
        copies[-1].start()
    own = part_ref[sta]
    whole = own
    for k, copy in enumerate(copies):
        copy.wait_recv()
        whole = whole + held[k]
    row_id = lax.broadcasted_iota(jnp.int32, whole.shape, 1)
    out_ref[0] = jnp.where(
        row_id < share, sharpness * (whole / whole[:, share : share + 1, :]), own
    )
    later = []
    for k in range(1, n_tmpl):
        later.append(
            pltpu.make_async_remote_copy(
                src_ref=out_ref.at[0],
                dst_ref=out_ref.at[k],
                send_sem=send_b.at[k - 1],
                recv_sem=recv_b.at[k - 1],
                device_id={"tmpl": lax.rem(tmpl + k, n_tmpl)},
                device_id_type=pl.DeviceIdType.MESH,
            )
        )
        later[-1].start()
    for copy in copies:
        copy.wait_send()
    for copy in later:
        copy.wait()


def all_scores(records, templates, channel_valid, shifts, hypo_id, hypo_xyz):
    stations, comps, samples = records.shape
    temps, taps = templates.shape[0], templates.shape[-1]
    rows = samples // LANES
    prows = -(-(rows + 1) // 8) * 8
    total = stations * comps * prows
    group = math.gcd(stations, 16)
    chans = group * comps
    unroll = math.gcd(stations, 12)
    assert temps % 2 == 0 and LANES - HALF + 1 < taps < LANES
    n_sta, n_tmpl = lax.axis_size("sta"), lax.axis_size("tmpl")
    out_rows = SAMPLES // LANES
    chunk_rows = -(-(out_rows // n_sta + 2) // 8) * 8
    axes, hypos = hypo_xyz.shape
    block = (temps, chunk_rows, LANES)
    return pl.pallas_call(
        functools.partial(trace_kernel, taps, group, chans, unroll, n_sta, n_tmpl),
        out_shape=jax.ShapeDtypeStruct((n_tmpl,) + block, jnp.float32),
        in_specs=[pl.BlockSpec(memory_space=pltpu.HBM)] * 6,
        out_specs=pl.BlockSpec(memory_space=pltpu.VMEM),
        scratch_shapes=[
            pltpu.SMEM((temps, stations), jnp.int32),
            pltpu.SMEM((comps, temps, stations), jnp.int32),
            pltpu.SMEM((temps,), jnp.int32),
            pltpu.VMEM((axes, hypos), jnp.float32),
            pltpu.VMEM((comps, stations, samples), jnp.bfloat16),
            pltpu.VMEM((temps, comps, stations, taps), jnp.bfloat16),
            pltpu.VMEM((total + 8, LANES), jnp.float32),
            pltpu.VMEM((stations * comps, 2 * prows, 2 * LANES), jnp.bfloat16),
            pltpu.VMEM((stations * comps, 2 * prows, LANES), jnp.float32),
            pltpu.VMEM((comps * temps * stations, LANES), jnp.float32),
            pltpu.VMEM((temps, out_rows, LANES), jnp.float32),
            pltpu.VMEM((unroll, temps, prows, LANES), jnp.float32),
            pltpu.VMEM((n_sta,) + block, jnp.float32),
            pltpu.VMEM((n_sta - 1,) + block, jnp.float32),
            pltpu.SemaphoreType.DMA((5,)),
            pltpu.SemaphoreType.DMA((stations // group,)),
            pltpu.SemaphoreType.DMA((n_sta - 1,)),
            pltpu.SemaphoreType.DMA((n_sta - 1,)),
            pltpu.SemaphoreType.DMA((n_tmpl - 1,)),
            pltpu.SemaphoreType.DMA((n_tmpl - 1,)),
        ],
        compiler_params=pltpu.CompilerParams(
            vmem_limit_bytes=60 * 2**20, collective_id=0, has_side_effects=True
        ),
        name="traces",
    )(
        shifts,
        jnp.transpose(channel_valid, (2, 0, 1)),
        hypo_id,
        hypo_xyz,
        jnp.transpose(records, (1, 0, 2)),
        jnp.transpose(templates, (0, 2, 1, 3)),
    )


def finish_kernel(
    share, axes, score_ref, best_hbm, evidence_hbm, place_hbm,
    best_ref, evidence_ref, place_ref, sem
):
    groups, temps = score_ref.shape[:2]
    pieces = [score_ref[n, t] for n in range(groups) for t in range(temps)]
    best = pieces[0]
    for piece in pieces[1:]:
        best = jnp.maximum(best, piece)
    best_ref[...] = best[:share]
    copies = [pltpu.make_async_copy(best_ref, best_hbm, sem.at[0])]
    copies[-1].start()
    total = jnp.zeros_like(best)
    sums = [jnp.zeros_like(best) for _ in range(axes)]
    for piece in pieces:
        weight = jnp.exp(piece - best)
        total = total + weight
        for j in range(axes):
            sums[j] = sums[j] + weight * piece[share + 1 : share + 2, j : j + 1]
    evidence_ref[...] = (best + jnp.log(total))[:share]
    copies.append(pltpu.make_async_copy(evidence_ref, evidence_hbm, sem.at[1]))
    copies[-1].start()
    for j in range(axes):
        located = sums[j] / total
        for r in range(share):
            place_ref[pl.ds(j, 1), pl.ds(r * LANES, LANES)] = located[r : r + 1]
    copies.append(pltpu.make_async_copy(place_ref, place_hbm, sem.at[2]))
    copies[-1].start()
    for copy in copies:
        copy.wait()


def on_device(records, templates, channel_valid, shifts, hypo_id, hypo_xyz):
    scores = all_scores(records, templates, channel_valid, shifts, hypo_id, hypo_xyz)
    axes = hypo_xyz.shape[0]
    share = SAMPLES // LANES // lax.axis_size("sta")
    hbm = pl.BlockSpec(memory_space=pltpu.HBM)
    shapes = ((share, LANES), (share, LANES), (axes, share * LANES))
    best, evidence, location = pl.pallas_call(
        functools.partial(finish_kernel, share, axes),
        out_shape=tuple(jax.ShapeDtypeStruct(shape, jnp.float32) for shape in shapes),
        in_specs=[pl.BlockSpec(memory_space=pltpu.VMEM)],
        out_specs=(hbm, hbm, hbm),
        scratch_shapes=[pltpu.VMEM(shape, jnp.float32) for shape in shapes]
        + [pltpu.SemaphoreType.DMA((3,))],
        name="finish",
    )(scores)
    return (best.reshape(-1), evidence.reshape(-1), location)


def solution(mesh):
    return jax.shard_map(
        on_device,
        mesh=mesh,
        in_specs=(
            P(("win", "sta"), None, None),
            P(("win", "tmpl"), "sta", None, None),
            P(("win", "tmpl"), "sta", None),
            P(("win", "tmpl"), "sta"),
            P(("win", "tmpl")),
            P(),
        ),
        out_specs=(P(("win", "sta")), P(("win", "sta")), P(None, ("win", "sta"))),
        check_vma=False,
    )
```

```python
import functools
import math

import jax
import jax.numpy as jnp
from jax import lax
from jax.experimental import pallas as pl
from jax.experimental.pallas import tpu as pltpu
from jax.sharding import PartitionSpec as P

SAMPLES = 3072

sharpness = 400.0
epsilon = 1e-06
LANES = 128


def trace_kernel(
    taps, group, unroll, n_sta, n_tmpl,
    shift_hbm, valid_hbm, hypo_hbm, place_hbm, x_hbm, w_hbm, out_ref,
    shift_ref, valid_ref, hypo_ref, place_ref, x_ref, w_ref,
    xs, xw, rn, ws, acc, scr, part_ref, held,
    sem_in, sem_x, send_a, recv_a, send_b, recv_b
):
    comps, stations, samples = x_ref.shape
    chunks, temps, chunk_rows = part_ref.shape[:3]
    sta, tmpl = lax.axis_index("sta"), lax.axis_index("tmpl")
    barrier = pltpu.get_barrier_semaphore()
    for axis, me, size in (("sta", sta, n_sta), ("tmpl", tmpl, n_tmpl)):
        for k in range(1, size):
            pl.semaphore_signal(
                barrier, inc=1, device_id={axis: lax.rem(me + k, size)},
                device_id_type=pl.DeviceIdType.MESH,
            )
    w_copy = pltpu.make_async_copy(w_hbm, w_ref, sem_in.at[0])
    w_copy.start()
    x_copies = []
    for g in range(stations // group):
        span = pl.ds(g * group, group)
        x_copies.append(
            pltpu.make_async_copy(x_hbm.at[:, span, :], x_ref.at[:, span, :], sem_x.at[g])
        )
        x_copies[-1].start()
    small = []
    for n, (src, dst) in enumerate(
        (
            (shift_hbm, shift_ref), (valid_hbm, valid_ref),
            (hypo_hbm, hypo_ref), (place_hbm, place_ref),
        )
    ):
        small.append(pltpu.make_async_copy(src, dst, sem_in.at[n + 1]))
        small[-1].start()
    out_rows = acc.shape[1]
    rows = samples // LANES
    prows = -(-(rows + 1) // 8) * 8
    srows = comps * prows
    j_id = lax.broadcasted_iota(jnp.int32, (LANES, LANES), 0)
    i_id = lax.broadcasted_iota(jnp.int32, (LANES, LANES), 1)
    upper = j_id >= i_id
    gap = j_id - i_id
    band = jnp.concatenate(
        [
            jnp.where((gap >= 0) & (gap < taps), 1.0, 0.0),
            jnp.where(gap + LANES < taps, 1.0, 0.0),
        ],
        axis=1,
    )
    band = jnp.concatenate([band, band], axis=0).astype(jnp.bfloat16)

    k_id = lax.broadcasted_iota(jnp.int32, (taps, LANES), 0)
    l_id = lax.broadcasted_iota(jnp.int32, (taps, LANES), 1)
    turn = jnp.where(lax.bitwise_and(k_id + l_id, LANES - 1) == 0, 1.0, 0.0).astype(jnp.bfloat16)
    w_copy.wait()
    for c in range(comps):
        for t in range(temps):
            wide = w_ref[t, c].astype(jnp.float32)
            power = jnp.sum(wide * wide, axis=-1, keepdims=True) / taps
            normed = (wide / (taps * jnp.sqrt(power + epsilon))).astype(jnp.bfloat16)
            ws[pl.ds((c * temps + t) * stations, stations), :] = jnp.dot(
                normed, turn, preferred_element_type=jnp.float32
            )

    xs[pl.ds(stations * srows, 8), :] = jnp.zeros((8, LANES), jnp.float32)

    def prepare(g, _):
        base = g * (group * srows)
        first = g * group
        for k in range(group * comps):
            xs[pl.ds(base + k * prows + prows - 8, 8), :] = jnp.zeros((8, LANES), jnp.float32)
        for c in range(comps):
            wave = x_ref[c, pl.ds(first, group), :].astype(jnp.float32)
            for r in range(rows):
                xs[pl.ds(base + c * prows + r, group, stride=srows), :] = wave[
                    :, r * LANES : (r + 1) * LANES
                ]
        count = group * srows
        here = xs[pl.ds(base, count), :]
        after = xs[pl.ds(base + 1, count), :]
        window = jnp.concatenate([here, after], axis=1)
        xw[pl.ds(base, count), :] = window.astype(jnp.bfloat16)
        square = here * here
        high = square.astype(jnp.bfloat16)
        low = (square - high.astype(jnp.float32)).astype(jnp.bfloat16)
        both = jnp.dot(
            jnp.concatenate([high, low], axis=1), band, preferred_element_type=jnp.float32
        )
        energy = both[:, :LANES] + pltpu.roll(both[:, LANES:], count - 1, 0)
        rn[pl.ds(base, count), :] = lax.rsqrt(energy * (1.0 / taps) + epsilon)
        return 0

    for g, copy in enumerate(x_copies):
        copy.wait()
        prepare(g, 0)
    for copy in small:
        copy.wait()

    lane = lax.broadcasted_iota(jnp.int32, (out_rows, LANES), 1)

    def one_station(s, slot, counts, moved):
        sums = [None] * temps
        counts, moved = list(counts), list(moved)
        for c in range(comps):
            base = pl.multiple_of((s * comps + c) * prows, 16)
            data = xw[pl.ds(base, prows), :]
            inverse = rn[pl.ds(base, prows), :]
            tiles = []
            for t in range(temps):
                valid = valid_ref[c, t, s]
                counts[t] = counts[t] + valid
                row = ws[pl.ds((c * temps + t) * stations + s, 1), :] * valid.astype(jnp.float32)
                ring = pltpu.roll(
                    jnp.broadcast_to(row, (LANES, LANES)), 0, 1, stride=1, stride_axis=0
                )
                tiles.append(
                    jnp.concatenate(
                        [jnp.where(upper, ring, 0.0), jnp.where(upper, 0.0, ring)], axis=0
                    ).astype(jnp.bfloat16)
                )
            raw = jnp.dot(
                data, jnp.concatenate(tiles, axis=1), preferred_element_type=jnp.float32
            )
            for t in range(temps):
                term = raw[:, t * LANES : (t + 1) * LANES] * inverse
                sums[t] = term if sums[t] is None else sums[t] + term
        for t in range(temps):
            shift = shift_ref[t, s]
            whole = lax.shift_right_logical(shift, 7)
            part = lax.bitwise_and(shift, LANES - 1)
            scr[slot, t] = pltpu.roll(
                sums[t], lax.bitwise_and(LANES - part, LANES - 1), 1
            )
            near = scr[slot, t, pl.ds(whole, out_rows), :]
            far = scr[slot, t, pl.ds(whole + 1, out_rows), :]
            moved[t] = moved[t] + jnp.where(lane < LANES - part, near, far)
        return counts, moved

    acc[...] = jnp.zeros_like(acc)

    def some_stations(g, counts):
        moved = [acc[t] for t in range(temps)]
        for k in range(unroll):
            counts, moved = one_station(g * unroll + k, k, counts, moved)
        for t in range(temps):
            acc[t] = moved[t]
        return tuple(counts)

    counts = lax.fori_loop(
        0, stations // unroll, some_stations, tuple(jnp.int32(0) for _ in range(temps))
    )

    share = out_rows // chunks
    axes, hypos = place_ref.shape
    h_id = lax.broadcasted_iota(jnp.int32, (axes, hypos), 1)
    row_id = lax.broadcasted_iota(jnp.int32, (axes, LANES), 0)
    col_id = lax.broadcasted_iota(jnp.int32, (axes, LANES), 1)
    for t in range(temps):
        place = jnp.sum(
            jnp.where(h_id == hypo_ref[t], place_ref[...], 0.0), axis=1, keepdims=True
        )
        place_row = jnp.sum(jnp.where(row_id == col_id, place, 0.0), axis=0, keepdims=True)
        count_row = jnp.full((1, LANES), counts[t].astype(jnp.float32))
        for b in range(chunks):
            part_ref[b, t, pl.ds(0, share), :] = acc[t, pl.ds(b * share, share), :]
            part_ref[b, t, pl.ds(share, 1), :] = count_row
            part_ref[b, t, pl.ds(share + 1, 1), :] = place_row
            if chunk_rows > share + 2:
                part_ref[b, t, pl.ds(share + 2, chunk_rows - share - 2), :] = jnp.zeros(
                    (chunk_rows - share - 2, LANES), jnp.float32
                )

    pl.semaphore_wait(barrier, n_sta + n_tmpl - 2)
    copies = []
    for k in range(1, n_sta):
        peer = lax.rem(sta + k, n_sta)
        copies.append(
            pltpu.make_async_remote_copy(
                src_ref=part_ref.at[peer],
                dst_ref=held.at[k - 1],
                send_sem=send_a.at[k - 1],
                recv_sem=recv_a.at[k - 1],
                device_id={"sta": peer},
                device_id_type=pl.DeviceIdType.MESH,
            )
        )
        copies[-1].start()
    own = part_ref[sta]
    whole = own
    for k, copy in enumerate(copies):
        copy.wait_recv()
        whole = whole + held[k]
    row_id = lax.broadcasted_iota(jnp.int32, whole.shape, 1)
    out_ref[0] = jnp.where(
        row_id < share, sharpness * (whole / whole[:, share : share + 1, :]), own
    )
    later = []
    for k in range(1, n_tmpl):
        later.append(
            pltpu.make_async_remote_copy(
                src_ref=out_ref.at[0],
                dst_ref=out_ref.at[k],
                send_sem=send_b.at[k - 1],
                recv_sem=recv_b.at[k - 1],
                device_id={"tmpl": lax.rem(tmpl + k, n_tmpl)},
                device_id_type=pl.DeviceIdType.MESH,
            )
        )
        later[-1].start()
    for copy in copies:
        copy.wait_send()
    for copy in later:
        copy.wait()


def all_scores(records, templates, channel_valid, shifts, hypo_id, hypo_xyz):
    stations, comps, samples = records.shape
    temps, taps = templates.shape[0], templates.shape[-1]
    rows = samples // LANES
    prows = -(-(rows + 1) // 8) * 8
    total = stations * comps * prows
    group = math.gcd(stations, 16)
    unroll = math.gcd(stations, 12)
    n_sta, n_tmpl = lax.axis_size("sta"), lax.axis_size("tmpl")
    out_rows = SAMPLES // LANES
    chunk_rows = -(-(out_rows // n_sta + 2) // 8) * 8
    axes, hypos = hypo_xyz.shape
    block = (temps, chunk_rows, LANES)
    return pl.pallas_call(
        functools.partial(trace_kernel, taps, group, unroll, n_sta, n_tmpl),
        out_shape=jax.ShapeDtypeStruct((n_tmpl,) + block, jnp.float32),
        in_specs=[pl.BlockSpec(memory_space=pltpu.HBM)] * 6,
        out_specs=pl.BlockSpec(memory_space=pltpu.VMEM),
        scratch_shapes=[
            pltpu.SMEM((temps, stations), jnp.int32),
            pltpu.SMEM((comps, temps, stations), jnp.int32),
            pltpu.SMEM((temps,), jnp.int32),
            pltpu.VMEM((axes, hypos), jnp.float32),
            pltpu.VMEM((comps, stations, samples), jnp.bfloat16),
            pltpu.VMEM((temps, comps, stations, taps), jnp.bfloat16),
            pltpu.VMEM((total + 8, LANES), jnp.float32),
            pltpu.VMEM((total, 2 * LANES), jnp.bfloat16),
            pltpu.VMEM((total, LANES), jnp.float32),
            pltpu.VMEM((comps * temps * stations, LANES), jnp.float32),
            pltpu.VMEM((temps, out_rows, LANES), jnp.float32),
            pltpu.VMEM((unroll, temps, prows, LANES), jnp.float32),
            pltpu.VMEM((n_sta,) + block, jnp.float32),
            pltpu.VMEM((n_sta - 1,) + block, jnp.float32),
            pltpu.SemaphoreType.DMA((5,)),
            pltpu.SemaphoreType.DMA((stations // group,)),
            pltpu.SemaphoreType.DMA((n_sta - 1,)),
            pltpu.SemaphoreType.DMA((n_sta - 1,)),
            pltpu.SemaphoreType.DMA((n_tmpl - 1,)),
            pltpu.SemaphoreType.DMA((n_tmpl - 1,)),
        ],
        compiler_params=pltpu.CompilerParams(
            vmem_limit_bytes=60 * 2**20, collective_id=0, has_side_effects=True
        ),
        name="traces",
    )(
        shifts,
        jnp.transpose(channel_valid, (2, 0, 1)),
        hypo_id,
        hypo_xyz,
        jnp.transpose(records, (1, 0, 2)),
        jnp.transpose(templates, (0, 2, 1, 3)),
    )


def finish_kernel(
    share, axes, score_ref, best_hbm, evidence_hbm, place_hbm,
    best_ref, evidence_ref, place_ref, sem
):
    groups, temps = score_ref.shape[:2]
    pieces = [score_ref[n, t] for n in range(groups) for t in range(temps)]
    best = pieces[0]
    for piece in pieces[1:]:
        best = jnp.maximum(best, piece)
    best_ref[...] = best[:share]
    copies = [pltpu.make_async_copy(best_ref, best_hbm, sem.at[0])]
    copies[-1].start()
    total = jnp.zeros_like(best)
    sums = [jnp.zeros_like(best) for _ in range(axes)]
    for piece in pieces:
        weight = jnp.exp(piece - best)
        total = total + weight
        for j in range(axes):
            sums[j] = sums[j] + weight * piece[share + 1 : share + 2, j : j + 1]
    evidence_ref[...] = (best + jnp.log(total))[:share]
    copies.append(pltpu.make_async_copy(evidence_ref, evidence_hbm, sem.at[1]))
    copies[-1].start()
    for j in range(axes):
        located = sums[j] / total
        for r in range(share):
            place_ref[pl.ds(j, 1), pl.ds(r * LANES, LANES)] = located[r : r + 1]
    copies.append(pltpu.make_async_copy(place_ref, place_hbm, sem.at[2]))
    copies[-1].start()
    for copy in copies:
        copy.wait()


def on_device(records, templates, channel_valid, shifts, hypo_id, hypo_xyz):
    scores = all_scores(records, templates, channel_valid, shifts, hypo_id, hypo_xyz)
    axes = hypo_xyz.shape[0]
    share = SAMPLES // LANES // lax.axis_size("sta")
    hbm = pl.BlockSpec(memory_space=pltpu.HBM)
    shapes = ((share, LANES), (share, LANES), (axes, share * LANES))
    best, evidence, location = pl.pallas_call(
        functools.partial(finish_kernel, share, axes),
        out_shape=tuple(jax.ShapeDtypeStruct(shape, jnp.float32) for shape in shapes),
        in_specs=[pl.BlockSpec(memory_space=pltpu.VMEM)],
        out_specs=(hbm, hbm, hbm),
        scratch_shapes=[pltpu.VMEM(shape, jnp.float32) for shape in shapes]
        + [pltpu.SemaphoreType.DMA((3,))],
        name="finish",
    )(scores)
    return (best.reshape(-1), evidence.reshape(-1), location)


def solution(mesh):
    return jax.shard_map(
        on_device,
        mesh=mesh,
        in_specs=(
            P(("win", "sta"), None, None),
            P(("win", "tmpl"), "sta", None, None),
            P(("win", "tmpl"), "sta", None),
            P(("win", "tmpl"), "sta"),
            P(("win", "tmpl")),
            P(),
        ),
        out_specs=(P(("win", "sta")), P(("win", "sta")), P(None, ("win", "sta"))),
        check_vma=False,
    )
```

```python
import functools
import math

import jax
import jax.numpy as jnp
from jax import lax
from jax.experimental import pallas as pl
from jax.experimental.pallas import tpu as pltpu
from jax.sharding import PartitionSpec as P

SAMPLES = 3072

sharpness = 400.0
epsilon = 1e-06
LANES = 128


def trace_kernel(
    taps, group, unroll, n_sta, n_tmpl,
    shift_hbm, valid_hbm, hypo_hbm, place_hbm, x_hbm, w_hbm, out_ref,
    shift_ref, valid_ref, hypo_ref, place_ref, x_ref, w_ref,
    xs, xw, rn, ws, acc, scr, part_ref, held,
    sem_in, sem_x, send_a, recv_a, send_b, recv_b
):
    comps, stations, samples = x_ref.shape
    chunks, temps, chunk_rows = part_ref.shape[:3]
    sta, tmpl = lax.axis_index("sta"), lax.axis_index("tmpl")
    barrier = pltpu.get_barrier_semaphore()
    for axis, me, size in (("sta", sta, n_sta), ("tmpl", tmpl, n_tmpl)):
        for k in range(1, size):
            pl.semaphore_signal(
                barrier, inc=1, device_id={axis: lax.rem(me + k, size)},
                device_id_type=pl.DeviceIdType.MESH,
            )
    w_copy = pltpu.make_async_copy(w_hbm, w_ref, sem_in.at[0])
    w_copy.start()
    x_copies = []
    for g in range(stations // group):
        span = pl.ds(g * group, group)
        x_copies.append(
            pltpu.make_async_copy(x_hbm.at[:, span, :], x_ref.at[:, span, :], sem_x.at[g])
        )
        x_copies[-1].start()
    small = []
    for n, (src, dst) in enumerate(
        (
            (shift_hbm, shift_ref), (valid_hbm, valid_ref),
            (hypo_hbm, hypo_ref), (place_hbm, place_ref),
        )
    ):
        small.append(pltpu.make_async_copy(src, dst, sem_in.at[n + 1]))
        small[-1].start()
    out_rows = acc.shape[1]
    rows = samples // LANES
    prows = -(-(rows + 1) // 8) * 8
    srows = comps * prows
    j_id = lax.broadcasted_iota(jnp.int32, (LANES, LANES), 0)
    i_id = lax.broadcasted_iota(jnp.int32, (LANES, LANES), 1)
    upper = jnp.where(j_id >= i_id, 1.0, 0.0).astype(jnp.bfloat16)
    lower = jnp.where(j_id < i_id, 1.0, 0.0).astype(jnp.bfloat16)
    gap = j_id - i_id
    band = jnp.concatenate(
        [
            jnp.where((gap >= 0) & (gap < taps), 1.0, 0.0),
            jnp.where(gap + LANES < taps, 1.0, 0.0),
        ],
        axis=1,
    )
    band = jnp.concatenate([band, band], axis=0).astype(jnp.bfloat16)

    k_id = lax.broadcasted_iota(jnp.int32, (taps, LANES), 0)
    l_id = lax.broadcasted_iota(jnp.int32, (taps, LANES), 1)
    turn = jnp.where(lax.bitwise_and(k_id + l_id, LANES - 1) == 0, 1.0, 0.0).astype(jnp.bfloat16)
    w_copy.wait()
    for c in range(comps):
        for t in range(temps):
            wide = w_ref[t, c].astype(jnp.float32)
            power = jnp.sum(wide * wide, axis=-1, keepdims=True) / taps
            normed = (wide / (taps * jnp.sqrt(power + epsilon))).astype(jnp.bfloat16)
            ws[pl.ds((c * temps + t) * stations, stations), :] = jnp.dot(
                normed, turn, preferred_element_type=jnp.float32
            )

    xs[pl.ds(stations * srows, 8), :] = jnp.zeros((8, LANES), jnp.float32)

    def prepare(g, _):
        base = g * (group * srows)
        first = g * group
        for k in range(group * comps):
            xs[pl.ds(base + k * prows + prows - 8, 8), :] = jnp.zeros((8, LANES), jnp.float32)
        for c in range(comps):
            wave = x_ref[c, pl.ds(first, group), :].astype(jnp.float32)
            for r in range(rows):
                xs[pl.ds(base + c * prows + r, group, stride=srows), :] = wave[
                    :, r * LANES : (r + 1) * LANES
                ]
        count = group * srows
        here = xs[pl.ds(base, count), :]
        after = xs[pl.ds(base + 1, count), :]
        window = jnp.concatenate([here, after], axis=1)
        xw[pl.ds(base, count), :] = window.astype(jnp.bfloat16)
        square = here * here
        high = square.astype(jnp.bfloat16)
        low = (square - high.astype(jnp.float32)).astype(jnp.bfloat16)
        both = jnp.dot(
            jnp.concatenate([high, low], axis=1), band, preferred_element_type=jnp.float32
        )
        energy = both[:, :LANES] + pltpu.roll(both[:, LANES:], count - 1, 0)
        rn[pl.ds(base, count), :] = lax.rsqrt(energy * (1.0 / taps) + epsilon)
        return 0

    for g, copy in enumerate(x_copies):
        copy.wait()
        prepare(g, 0)
    for copy in small:
        copy.wait()

    lane = lax.broadcasted_iota(jnp.int32, (out_rows, LANES), 1)

    def one_station(s, slot, counts, moved):
        sums = [None] * temps
        counts, moved = list(counts), list(moved)
        for c in range(comps):
            base = pl.multiple_of((s * comps + c) * prows, 16)
            data = xw[pl.ds(base, prows), :]
            inverse = rn[pl.ds(base, prows), :]
            tiles = []
            for t in range(temps):
                valid = valid_ref[c, t, s]
                counts[t] = counts[t] + valid
                row = ws[pl.ds((c * temps + t) * stations + s, 1), :] * valid.astype(jnp.float32)
                ring = pltpu.roll(
                    jnp.broadcast_to(row, (LANES, LANES)), 0, 1, stride=1, stride_axis=0
                ).astype(jnp.bfloat16)
                tiles.append(jnp.concatenate([ring * upper, ring * lower], axis=0))
            raw = jnp.dot(
                data, jnp.concatenate(tiles, axis=1), preferred_element_type=jnp.float32
            )
            for t in range(temps):
                term = raw[:, t * LANES : (t + 1) * LANES] * inverse
                sums[t] = term if sums[t] is None else sums[t] + term
        for t in range(temps):
            shift = shift_ref[t, s]
            whole = lax.shift_right_logical(shift, 7)
            part = lax.bitwise_and(shift, LANES - 1)
            scr[slot, t] = pltpu.roll(
                sums[t], lax.bitwise_and(LANES - part, LANES - 1), 1
            )
            near = scr[slot, t, pl.ds(whole, out_rows), :]
            far = scr[slot, t, pl.ds(whole + 1, out_rows), :]
            moved[t] = moved[t] + jnp.where(lane < LANES - part, near, far)
        return counts, moved

    acc[...] = jnp.zeros_like(acc)

    def some_stations(g, counts):
        moved = [acc[t] for t in range(temps)]
        for k in range(unroll):
            counts, moved = one_station(g * unroll + k, k, counts, moved)
        for t in range(temps):
            acc[t] = moved[t]
        return tuple(counts)

    counts = lax.fori_loop(
        0, stations // unroll, some_stations, tuple(jnp.int32(0) for _ in range(temps))
    )

    share = out_rows // chunks
    axes, hypos = place_ref.shape
    h_id = lax.broadcasted_iota(jnp.int32, (axes, hypos), 1)
    row_id = lax.broadcasted_iota(jnp.int32, (axes, LANES), 0)
    col_id = lax.broadcasted_iota(jnp.int32, (axes, LANES), 1)
    for t in range(temps):
        place = jnp.sum(
            jnp.where(h_id == hypo_ref[t], place_ref[...], 0.0), axis=1, keepdims=True
        )
        place_row = jnp.sum(jnp.where(row_id == col_id, place, 0.0), axis=0, keepdims=True)
        count_row = jnp.full((1, LANES), counts[t].astype(jnp.float32))
        for b in range(chunks):
            part_ref[b, t, pl.ds(0, share), :] = acc[t, pl.ds(b * share, share), :]
            part_ref[b, t, pl.ds(share, 1), :] = count_row
            part_ref[b, t, pl.ds(share + 1, 1), :] = place_row
            if chunk_rows > share + 2:
                part_ref[b, t, pl.ds(share + 2, chunk_rows - share - 2), :] = jnp.zeros(
                    (chunk_rows - share - 2, LANES), jnp.float32
                )

    pl.semaphore_wait(barrier, n_sta + n_tmpl - 2)
    copies = []
    for k in range(1, n_sta):
        peer = lax.rem(sta + k, n_sta)
        copies.append(
            pltpu.make_async_remote_copy(
                src_ref=part_ref.at[peer],
                dst_ref=held.at[k - 1],
                send_sem=send_a.at[k - 1],
                recv_sem=recv_a.at[k - 1],
                device_id={"sta": peer},
                device_id_type=pl.DeviceIdType.MESH,
            )
        )
        copies[-1].start()
    own = part_ref[sta]
    whole = own
    for k, copy in enumerate(copies):
        copy.wait_recv()
        whole = whole + held[k]
    row_id = lax.broadcasted_iota(jnp.int32, whole.shape, 1)
    out_ref[0] = jnp.where(
        row_id < share, sharpness * (whole / whole[:, share : share + 1, :]), own
    )
    later = []
    for k in range(1, n_tmpl):
        later.append(
            pltpu.make_async_remote_copy(
                src_ref=out_ref.at[0],
                dst_ref=out_ref.at[k],
                send_sem=send_b.at[k - 1],
                recv_sem=recv_b.at[k - 1],
                device_id={"tmpl": lax.rem(tmpl + k, n_tmpl)},
                device_id_type=pl.DeviceIdType.MESH,
            )
        )
        later[-1].start()
    for copy in copies:
        copy.wait_send()
    for copy in later:
        copy.wait()


def all_scores(records, templates, channel_valid, shifts, hypo_id, hypo_xyz):
    stations, comps, samples = records.shape
    temps, taps = templates.shape[0], templates.shape[-1]
    rows = samples // LANES
    prows = -(-(rows + 1) // 8) * 8
    total = stations * comps * prows
    group = math.gcd(stations, 16)
    unroll = math.gcd(stations, 16)
    n_sta, n_tmpl = lax.axis_size("sta"), lax.axis_size("tmpl")
    out_rows = SAMPLES // LANES
    chunk_rows = -(-(out_rows // n_sta + 2) // 8) * 8
    axes, hypos = hypo_xyz.shape
    block = (temps, chunk_rows, LANES)
    return pl.pallas_call(
        functools.partial(trace_kernel, taps, group, unroll, n_sta, n_tmpl),
        out_shape=jax.ShapeDtypeStruct((n_tmpl,) + block, jnp.float32),
        in_specs=[pl.BlockSpec(memory_space=pltpu.HBM)] * 6,
        out_specs=pl.BlockSpec(memory_space=pltpu.VMEM),
        scratch_shapes=[
            pltpu.SMEM((temps, stations), jnp.int32),
            pltpu.SMEM((comps, temps, stations), jnp.int32),
            pltpu.SMEM((temps,), jnp.int32),
            pltpu.VMEM((axes, hypos), jnp.float32),
            pltpu.VMEM((comps, stations, samples), jnp.bfloat16),
            pltpu.VMEM((temps, comps, stations, taps), jnp.bfloat16),
            pltpu.VMEM((total + 8, LANES), jnp.float32),
            pltpu.VMEM((total, 2 * LANES), jnp.bfloat16),
            pltpu.VMEM((total, LANES), jnp.float32),
            pltpu.VMEM((comps * temps * stations, LANES), jnp.float32),
            pltpu.VMEM((temps, out_rows, LANES), jnp.float32),
            pltpu.VMEM((unroll, temps, prows, LANES), jnp.float32),
            pltpu.VMEM((n_sta,) + block, jnp.float32),
            pltpu.VMEM((n_sta - 1,) + block, jnp.float32),
            pltpu.SemaphoreType.DMA((5,)),
            pltpu.SemaphoreType.DMA((stations // group,)),
            pltpu.SemaphoreType.DMA((n_sta - 1,)),
            pltpu.SemaphoreType.DMA((n_sta - 1,)),
            pltpu.SemaphoreType.DMA((n_tmpl - 1,)),
            pltpu.SemaphoreType.DMA((n_tmpl - 1,)),
        ],
        compiler_params=pltpu.CompilerParams(
            vmem_limit_bytes=60 * 2**20, collective_id=0, has_side_effects=True
        ),
        name="traces",
    )(
        shifts,
        jnp.transpose(channel_valid, (2, 0, 1)),
        hypo_id,
        hypo_xyz,
        jnp.transpose(records, (1, 0, 2)),
        jnp.transpose(templates, (0, 2, 1, 3)),
    )


def finish_kernel(
    share, axes, score_ref, best_hbm, evidence_hbm, place_hbm,
    best_ref, evidence_ref, place_ref, sem
):
    groups, temps = score_ref.shape[:2]
    pieces = [score_ref[n, t] for n in range(groups) for t in range(temps)]
    best = pieces[0]
    for piece in pieces[1:]:
        best = jnp.maximum(best, piece)
    best_ref[...] = best[:share]
    copies = [pltpu.make_async_copy(best_ref, best_hbm, sem.at[0])]
    copies[-1].start()
    total = jnp.zeros_like(best)
    sums = [jnp.zeros_like(best) for _ in range(axes)]
    for piece in pieces:
        weight = jnp.exp(piece - best)
        total = total + weight
        for j in range(axes):
            sums[j] = sums[j] + weight * piece[share + 1 : share + 2, j : j + 1]
    evidence_ref[...] = (best + jnp.log(total))[:share]
    copies.append(pltpu.make_async_copy(evidence_ref, evidence_hbm, sem.at[1]))
    copies[-1].start()
    for j in range(axes):
        located = sums[j] / total
        for r in range(share):
            place_ref[pl.ds(j, 1), pl.ds(r * LANES, LANES)] = located[r : r + 1]
    copies.append(pltpu.make_async_copy(place_ref, place_hbm, sem.at[2]))
    copies[-1].start()
    for copy in copies:
        copy.wait()


def on_device(records, templates, channel_valid, shifts, hypo_id, hypo_xyz):
    scores = all_scores(records, templates, channel_valid, shifts, hypo_id, hypo_xyz)
    axes = hypo_xyz.shape[0]
    share = SAMPLES // LANES // lax.axis_size("sta")
    hbm = pl.BlockSpec(memory_space=pltpu.HBM)
    shapes = ((share, LANES), (share, LANES), (axes, share * LANES))
    best, evidence, location = pl.pallas_call(
        functools.partial(finish_kernel, share, axes),
        out_shape=tuple(jax.ShapeDtypeStruct(shape, jnp.float32) for shape in shapes),
        in_specs=[pl.BlockSpec(memory_space=pltpu.VMEM)],
        out_specs=(hbm, hbm, hbm),
        scratch_shapes=[pltpu.VMEM(shape, jnp.float32) for shape in shapes]
        + [pltpu.SemaphoreType.DMA((3,))],
        name="finish",
    )(scores)
    return (best.reshape(-1), evidence.reshape(-1), location)


def solution(mesh):
    return jax.shard_map(
        on_device,
        mesh=mesh,
        in_specs=(
            P(("win", "sta"), None, None),
            P(("win", "tmpl"), "sta", None, None),
            P(("win", "tmpl"), "sta", None),
            P(("win", "tmpl"), "sta"),
            P(("win", "tmpl")),
            P(),
        ),
        out_specs=(P(("win", "sta")), P(("win", "sta")), P(None, ("win", "sta"))),
        check_vma=False,
    )
```

```python
import functools
import math

import jax
import jax.numpy as jnp
from jax import lax
from jax.experimental import pallas as pl
from jax.experimental.pallas import tpu as pltpu
from jax.sharding import PartitionSpec as P

SAMPLES = 3072

sharpness = 400.0
epsilon = 1e-06
LANES = 128


def trace_kernel(
    taps, group, unroll, n_sta, n_tmpl,
    shift_hbm, valid_hbm, hypo_hbm, place_hbm, x_hbm, w_hbm, out_ref,
    shift_ref, valid_ref, hypo_ref, place_ref, x_ref, w_ref,
    xs, xw, rn, ws, acc, scr, part_ref, held,
    sem_in, sem_x, send_a, recv_a, send_b, recv_b
):
    comps, stations, samples = x_ref.shape
    chunks, temps, chunk_rows = part_ref.shape[:3]
    sta, tmpl = lax.axis_index("sta"), lax.axis_index("tmpl")
    barrier = pltpu.get_barrier_semaphore()
    for axis, me, size in (("sta", sta, n_sta), ("tmpl", tmpl, n_tmpl)):
        for k in range(1, size):
            pl.semaphore_signal(
                barrier, inc=1, device_id={axis: lax.rem(me + k, size)},
                device_id_type=pl.DeviceIdType.MESH,
            )
    w_copy = pltpu.make_async_copy(w_hbm, w_ref, sem_in.at[0])
    w_copy.start()
    x_copies = []
    for g in range(stations // group):
        span = pl.ds(g * group, group)
        x_copies.append(
            pltpu.make_async_copy(x_hbm.at[:, span, :], x_ref.at[:, span, :], sem_x.at[g])
        )
        x_copies[-1].start()
    small = []
    for n, (src, dst) in enumerate(
        (
            (shift_hbm, shift_ref), (valid_hbm, valid_ref),
            (hypo_hbm, hypo_ref), (place_hbm, place_ref),
        )
    ):
        small.append(pltpu.make_async_copy(src, dst, sem_in.at[n + 1]))
        small[-1].start()
    out_rows = acc.shape[1]
    rows = samples // LANES
    prows = -(-(rows + 1) // 8) * 8
    srows = comps * prows
    j_id = lax.broadcasted_iota(jnp.int32, (LANES, LANES), 0)
    i_id = lax.broadcasted_iota(jnp.int32, (LANES, LANES), 1)
    upper = jnp.where(j_id >= i_id, 1.0, 0.0).astype(jnp.bfloat16)
    lower = jnp.where(j_id < i_id, 1.0, 0.0).astype(jnp.bfloat16)
    gap = j_id - i_id
    band = jnp.concatenate(
        [
            jnp.where((gap >= 0) & (gap < taps), 1.0, 0.0),
            jnp.where(gap + LANES < taps, 1.0, 0.0),
        ],
        axis=1,
    )
    band = jnp.concatenate([band, band], axis=0).astype(jnp.bfloat16)

    k_id = lax.broadcasted_iota(jnp.int32, (taps, LANES), 0)
    l_id = lax.broadcasted_iota(jnp.int32, (taps, LANES), 1)
    turn = jnp.where(lax.bitwise_and(k_id + l_id, LANES - 1) == 0, 1.0, 0.0).astype(jnp.bfloat16)
    w_copy.wait()
    for c in range(comps):
        for t in range(temps):
            wide = w_ref[t, c].astype(jnp.float32)
            power = jnp.sum(wide * wide, axis=-1, keepdims=True) / taps
            normed = (wide / (taps * jnp.sqrt(power + epsilon))).astype(jnp.bfloat16)
            ws[pl.ds((c * temps + t) * stations, stations), :] = jnp.dot(
                normed, turn, preferred_element_type=jnp.float32
            )

    xs[pl.ds(stations * srows, 8), :] = jnp.zeros((8, LANES), jnp.float32)

    def prepare(g, _):
        base = g * (group * srows)
        first = g * group
        for k in range(group * comps):
            xs[pl.ds(base + k * prows + prows - 8, 8), :] = jnp.zeros((8, LANES), jnp.float32)
        for c in range(comps):
            wave = x_ref[c, pl.ds(first, group), :].astype(jnp.float32)
            for r in range(rows):
                xs[pl.ds(base + c * prows + r, group, stride=srows), :] = wave[
                    :, r * LANES : (r + 1) * LANES
                ]
        count = group * srows
        here = xs[pl.ds(base, count), :]
        after = xs[pl.ds(base + 1, count), :]
        window = jnp.concatenate([here, after], axis=1)
        xw[pl.ds(base, count), :] = window.astype(jnp.bfloat16)
        square = here * here
        high = square.astype(jnp.bfloat16)
        low = (square - high.astype(jnp.float32)).astype(jnp.bfloat16)
        both = jnp.dot(
            jnp.concatenate([high, low], axis=1), band, preferred_element_type=jnp.float32
        )
        energy = both[:, :LANES] + pltpu.roll(both[:, LANES:], count - 1, 0)
        rn[pl.ds(base, count), :] = lax.rsqrt(energy * (1.0 / taps) + epsilon)
        return 0


    lane = lax.broadcasted_iota(jnp.int32, (out_rows, LANES), 1)

    def one_station(s, slot, counts, moved):
        sums = [None] * temps
        counts, moved = list(counts), list(moved)
        for c in range(comps):
            base = (s * comps + c) * prows
            data = xw[pl.ds(base, prows), :]
            inverse = rn[pl.ds(base, prows), :]
            tiles = []
            for t in range(temps):
                valid = valid_ref[c, t, s]
                counts[t] = counts[t] + valid
                row = ws[pl.ds((c * temps + t) * stations + s, 1), :] * valid.astype(jnp.float32)
                ring = pltpu.roll(
                    jnp.broadcast_to(row, (LANES, LANES)), 0, 1, stride=1, stride_axis=0
                ).astype(jnp.bfloat16)
                tiles.append(jnp.concatenate([ring * upper, ring * lower], axis=0))
            raw = jnp.dot(
                data, jnp.concatenate(tiles, axis=1), preferred_element_type=jnp.float32
            )
            for t in range(temps):
                term = raw[:, t * LANES : (t + 1) * LANES] * inverse
                sums[t] = term if sums[t] is None else sums[t] + term
        for t in range(temps):
            shift = shift_ref[t, s]
            whole = lax.shift_right_logical(shift, 7)
            part = lax.bitwise_and(shift, LANES - 1)
            scr[slot, t] = pltpu.roll(
                sums[t], lax.bitwise_and(LANES - part, LANES - 1), 1
            )
            near = scr[slot, t, pl.ds(whole, out_rows), :]
            far = scr[slot, t, pl.ds(whole + 1, out_rows), :]
            moved[t] = moved[t] + jnp.where(lane < LANES - part, near, far)
        return counts, moved

    acc[...] = jnp.zeros_like(acc)

    def some_stations(g, counts):
        moved = [acc[t] for t in range(temps)]
        for k in range(unroll):
            counts, moved = one_station(g * unroll + k, k, counts, moved)
        for t in range(temps):
            acc[t] = moved[t]
        return tuple(counts)

    counts = tuple(jnp.int32(0) for _ in range(temps))
    for copy in small:
        copy.wait()
    for g, copy in enumerate(x_copies):
        copy.wait()
        prepare(g, 0)
        counts = some_stations(g, counts)

    share = out_rows // chunks
    axes, hypos = place_ref.shape
    h_id = lax.broadcasted_iota(jnp.int32, (axes, hypos), 1)
    row_id = lax.broadcasted_iota(jnp.int32, (axes, LANES), 0)
    col_id = lax.broadcasted_iota(jnp.int32, (axes, LANES), 1)
    for t in range(temps):
        place = jnp.sum(
            jnp.where(h_id == hypo_ref[t], place_ref[...], 0.0), axis=1, keepdims=True
        )
        place_row = jnp.sum(jnp.where(row_id == col_id, place, 0.0), axis=0, keepdims=True)
        count_row = jnp.full((1, LANES), counts[t].astype(jnp.float32))
        for b in range(chunks):
            part_ref[b, t, pl.ds(0, share), :] = acc[t, pl.ds(b * share, share), :]
            part_ref[b, t, pl.ds(share, 1), :] = count_row
            part_ref[b, t, pl.ds(share + 1, 1), :] = place_row
            if chunk_rows > share + 2:
                part_ref[b, t, pl.ds(share + 2, chunk_rows - share - 2), :] = jnp.zeros(
                    (chunk_rows - share - 2, LANES), jnp.float32
                )

    pl.semaphore_wait(barrier, n_sta + n_tmpl - 2)
    copies = []
    for k in range(1, n_sta):
        peer = lax.rem(sta + k, n_sta)
        copies.append(
            pltpu.make_async_remote_copy(
                src_ref=part_ref.at[peer],
                dst_ref=held.at[k - 1],
                send_sem=send_a.at[k - 1],
                recv_sem=recv_a.at[k - 1],
                device_id={"sta": peer},
                device_id_type=pl.DeviceIdType.MESH,
            )
        )
        copies[-1].start()
    own = part_ref[sta]
    whole = own
    for k, copy in enumerate(copies):
        copy.wait_recv()
        whole = whole + held[k]
    row_id = lax.broadcasted_iota(jnp.int32, whole.shape, 1)
    out_ref[0] = jnp.where(
        row_id < share, sharpness * (whole / whole[:, share : share + 1, :]), own
    )
    later = []
    for k in range(1, n_tmpl):
        later.append(
            pltpu.make_async_remote_copy(
                src_ref=out_ref.at[0],
                dst_ref=out_ref.at[k],
                send_sem=send_b.at[k - 1],
                recv_sem=recv_b.at[k - 1],
                device_id={"tmpl": lax.rem(tmpl + k, n_tmpl)},
                device_id_type=pl.DeviceIdType.MESH,
            )
        )
        later[-1].start()
    for copy in copies:
        copy.wait_send()
    for copy in later:
        copy.wait()


def all_scores(records, templates, channel_valid, shifts, hypo_id, hypo_xyz):
    stations, comps, samples = records.shape
    temps, taps = templates.shape[0], templates.shape[-1]
    rows = samples // LANES
    prows = -(-(rows + 1) // 8) * 8
    total = stations * comps * prows
    group = math.gcd(stations, 16)
    unroll = group
    n_sta, n_tmpl = lax.axis_size("sta"), lax.axis_size("tmpl")
    out_rows = SAMPLES // LANES
    chunk_rows = -(-(out_rows // n_sta + 2) // 8) * 8
    axes, hypos = hypo_xyz.shape
    block = (temps, chunk_rows, LANES)
    return pl.pallas_call(
        functools.partial(trace_kernel, taps, group, unroll, n_sta, n_tmpl),
        out_shape=jax.ShapeDtypeStruct((n_tmpl,) + block, jnp.float32),
        in_specs=[pl.BlockSpec(memory_space=pltpu.HBM)] * 6,
        out_specs=pl.BlockSpec(memory_space=pltpu.VMEM),
        scratch_shapes=[
            pltpu.SMEM((temps, stations), jnp.int32),
            pltpu.SMEM((comps, temps, stations), jnp.int32),
            pltpu.SMEM((temps,), jnp.int32),
            pltpu.VMEM((axes, hypos), jnp.float32),
            pltpu.VMEM((comps, stations, samples), jnp.bfloat16),
            pltpu.VMEM((temps, comps, stations, taps), jnp.bfloat16),
            pltpu.VMEM((total + comps * prows, LANES), jnp.float32),
            pltpu.VMEM((total, 2 * LANES), jnp.bfloat16),
            pltpu.VMEM((total, LANES), jnp.float32),
            pltpu.VMEM((comps * temps * stations, LANES), jnp.float32),
            pltpu.VMEM((temps, out_rows, LANES), jnp.float32),
            pltpu.VMEM((unroll, temps, prows, LANES), jnp.float32),
            pltpu.VMEM((n_sta,) + block, jnp.float32),
            pltpu.VMEM((n_sta - 1,) + block, jnp.float32),
            pltpu.SemaphoreType.DMA((5,)),
            pltpu.SemaphoreType.DMA((stations // group,)),
            pltpu.SemaphoreType.DMA((n_sta - 1,)),
            pltpu.SemaphoreType.DMA((n_sta - 1,)),
            pltpu.SemaphoreType.DMA((n_tmpl - 1,)),
            pltpu.SemaphoreType.DMA((n_tmpl - 1,)),
        ],
        compiler_params=pltpu.CompilerParams(
            vmem_limit_bytes=60 * 2**20, collective_id=0, has_side_effects=True
        ),
        name="traces",
    )(
        shifts,
        jnp.transpose(channel_valid, (2, 0, 1)),
        hypo_id,
        hypo_xyz,
        jnp.transpose(records, (1, 0, 2)),
        jnp.transpose(templates, (0, 2, 1, 3)),
    )


def finish_kernel(
    share, axes, score_ref, best_hbm, evidence_hbm, place_hbm,
    best_ref, evidence_ref, place_ref, sem
):
    groups, temps = score_ref.shape[:2]
    pieces = [score_ref[n, t] for n in range(groups) for t in range(temps)]
    best = pieces[0]
    for piece in pieces[1:]:
        best = jnp.maximum(best, piece)
    best_ref[...] = best[:share]
    copies = [pltpu.make_async_copy(best_ref, best_hbm, sem.at[0])]
    copies[-1].start()
    total = jnp.zeros_like(best)
    sums = [jnp.zeros_like(best) for _ in range(axes)]
    for piece in pieces:
        weight = jnp.exp(piece - best)
        total = total + weight
        for j in range(axes):
            sums[j] = sums[j] + weight * piece[share + 1 : share + 2, j : j + 1]
    evidence_ref[...] = (best + jnp.log(total))[:share]
    copies.append(pltpu.make_async_copy(evidence_ref, evidence_hbm, sem.at[1]))
    copies[-1].start()
    for j in range(axes):
        located = sums[j] / total
        for r in range(share):
            place_ref[pl.ds(j, 1), pl.ds(r * LANES, LANES)] = located[r : r + 1]
    copies.append(pltpu.make_async_copy(place_ref, place_hbm, sem.at[2]))
    copies[-1].start()
    for copy in copies:
        copy.wait()


def on_device(records, templates, channel_valid, shifts, hypo_id, hypo_xyz):
    scores = all_scores(records, templates, channel_valid, shifts, hypo_id, hypo_xyz)
    axes = hypo_xyz.shape[0]
    share = SAMPLES // LANES // lax.axis_size("sta")
    hbm = pl.BlockSpec(memory_space=pltpu.HBM)
    shapes = ((share, LANES), (share, LANES), (axes, share * LANES))
    best, evidence, location = pl.pallas_call(
        functools.partial(finish_kernel, share, axes),
        out_shape=tuple(jax.ShapeDtypeStruct(shape, jnp.float32) for shape in shapes),
        in_specs=[pl.BlockSpec(memory_space=pltpu.VMEM)],
        out_specs=(hbm, hbm, hbm),
        scratch_shapes=[pltpu.VMEM(shape, jnp.float32) for shape in shapes]
        + [pltpu.SemaphoreType.DMA((3,))],
        name="finish",
    )(scores)
    return (best.reshape(-1), evidence.reshape(-1), location)


def solution(mesh):
    return jax.shard_map(
        on_device,
        mesh=mesh,
        in_specs=(
            P(("win", "sta"), None, None),
            P(("win", "tmpl"), "sta", None, None),
            P(("win", "tmpl"), "sta", None),
            P(("win", "tmpl"), "sta"),
            P(("win", "tmpl")),
            P(),
        ),
        out_specs=(P(("win", "sta")), P(("win", "sta")), P(None, ("win", "sta"))),
        check_vma=False,
    )
```
